32 devices in a mesh: group: 8 (over y, x, core), narrow: 4 (over z).
Axes of the slice: x: 2, y: 2, z: 4, core: 2. Of those that a mesh axis runs over, the one named last changes fastest.
Arguments:
- patches: bfloat16 [512, 3675], P(('group', 'narrow')), may hold values from -8 to 8
- counts: int32 [512], P(('group', 'narrow')), may hold values from 1 to 49
- weights: float32 [49], replicated, may hold values from 0.3 to 3
- probes: float32 [512, 16], P(('group', 'narrow')), may hold values from -6 to 6
- plan: int32 [4, 8], replicated, may hold values from 0 to 7, as said below
Outputs:
- product: float32 [512, 16], P(('group', 'narrow'))
The draws below stay inside these ranges and needn't reach their ends.
Inputs may be any that keep to these rules, and one draw needn't show every extreme that they name: Each row pairs the 8 blocks: plan[m, plan[m, b]] = b and plan[m, b] != b.
All inputs are finite; a program needn't handle non-finite values.
Results may differ from the reference program's by a relative error of at most 0.008.
Values may be sent and summed in bfloat16 or wider, within the bound.
No kernel may reach another device: no remote copies, remote signals or barrier semaphores. Data moves between devices by JAX's collectives and lax.ppermute only.
A program may use at most 64 MiB of HBM per device.

```python
import math
import jax
import jax.numpy as jnp
from jax import lax

P_SIZE = 49
PV = 75
NPROBE = 16
MEET = 4
IMG_DEV = 16
NB = 64
NIMG = 512
N_GROUP = 8
N_NARROW = 4


def draw_patches(key, part):
    first, second, third = jax.random.split(key, 3)
    levels = jax.random.normal(first, (NIMG, P_SIZE, 8), jnp.float32)
    noise = jax.random.normal(third, (NIMG, P_SIZE, PV), jnp.float32)
    scales = jnp.exp(jax.random.uniform(second, (NIMG, P_SIZE, 1), jnp.float32, 0.0, jnp.log(2.1)))
    member = jnp.arange(PV, dtype=jnp.int32) * 8 // PV
    spread = jnp.take(levels * scales, member, axis=2)
    values = spread + 0.3 * noise
    return jnp.clip(values, -8.0, 8.0).reshape(NIMG, P_SIZE * PV).astype(jnp.bfloat16)


def draw_plan(key, part):
    rows = []
    for meeting in range(MEET):
        order = jax.random.permutation(jax.random.fold_in(key, meeting + 11), N_GROUP).astype(jnp.int32)
        left = order[0::2]
        right = order[1::2]
        partner = jnp.zeros((N_GROUP,), jnp.int32).at[left].set(right).at[right].set(left)
        rows.append(partner)
    return jnp.stack(rows, axis=0)


def plant(values, key, low, high):
    longest = values.shape.index(max(values.shape))
    spots = []
    for shift in (0, 1):
        where = [jax.random.randint(jax.random.fold_in(key, axis), (), 0, length) for axis, length in enumerate(values.shape)]
        where[longest] = (where[longest] + shift) % values.shape[longest]
        spots.append(tuple(where))
    return values.at[spots[0]].set(low).at[spots[1]].set(high)


def block_scale(own_key, shape, cuts, low, top_value):
    def one(dim, parts):
        steps = jax.random.uniform(jax.random.fold_in(jax.random.fold_in(own_key, 6), dim), (parts,), jnp.float32, low / len(cuts), top_value / len(cuts))
        return jnp.repeat(jnp.exp(steps), shape[dim] // parts).reshape((-1,) + (1,) * (len(shape) - dim - 1))

    level = one(*cuts[0])
    for cut in cuts[1:]:
        level = level * one(*cut)
    return level


def normal_values(rng, shape, width, reach, cuts=(), kind=jnp.bfloat16):
    values = jax.random.normal(rng, shape, jnp.float32) * width
    if len(cuts) > 0:
        values = block_scale(rng, shape, cuts, -0.22, 0.18) * values
    return jnp.clip(values, min=-reach, max=reach).astype(kind)


def setup_inputs(seed: int = 0) -> dict:
    key_list = jax.random.split(jax.random.key(seed), 6)
    return {
        "patches": draw_patches(jax.random.fold_in(key_list[5], 71), 0),
        "counts": plant(jax.random.randint(key_list[1], (NIMG,), 1, P_SIZE + 1), jax.random.fold_in(key_list[1], 1), 1, P_SIZE).astype(jnp.int32),
        "weights": jnp.clip(jnp.exp(jax.random.uniform(key_list[2], (P_SIZE,), jnp.float32, math.log(0.3), math.log(3.0))), 0.3, 3.0),
        "probes": normal_values(key_list[3], (NIMG, NPROBE), 1.0, 6.0, ((0, 32),), jnp.float32),
        "plan": draw_plan(jax.random.fold_in(key_list[5], 71), 0),
    }


def kernel_tile(rows_x, cols_x):
    inner = lax.dot_general(rows_x, cols_x, (((1,), (1,)), ((), ())), preferred_element_type=jnp.float32)
    rows_f = rows_x.astype(jnp.float32)
    cols_f = cols_x.astype(jnp.float32)
    rows_n = jnp.sum(rows_f * rows_f, axis=1)
    cols_n = jnp.sum(cols_f * cols_f, axis=1)
    return jnp.exp((2.0 * inner - rows_n[:, None] - cols_n[None, :]) / (2.0 * PV)).astype(jnp.bfloat16)


def reference(patches, counts, weights, probes, plan):
    span = IMG_DEV * P_SIZE
    every_x = patches.reshape(N_GROUP, NB * P_SIZE, PV)
    valid = (jnp.arange(P_SIZE, dtype=jnp.int32)[None, :] < counts[:, None]).astype(jnp.float32)
    alpha = weights[None, :] * valid / counts[:, None].astype(jnp.float32)
    every_u = (alpha[:, :, None] * probes[:, None, :]).astype(jnp.bfloat16).reshape(N_GROUP, NB * P_SIZE, NPROBE)
    every_a = alpha.reshape(N_GROUP, NB * P_SIZE)

    def one_group(block):
        rows_x = lax.dynamic_index_in_dim(every_x, block, 0, keepdims=False)
        rows_a = lax.dynamic_index_in_dim(every_a, block, 0, keepdims=False)
        total = jnp.zeros((NB * P_SIZE, NPROBE), jnp.float32)
        for meeting in range(MEET):
            partner = lax.dynamic_index_in_dim(plan[meeting], block, 0, keepdims=False)
            cols_x = lax.dynamic_index_in_dim(every_x, partner, 0, keepdims=False)
            cols_u = lax.dynamic_index_in_dim(every_u, partner, 0, keepdims=False)

            def add_sub(carry, index):
                start = (index * span).astype(jnp.int32)
                sub_x = lax.dynamic_slice_in_dim(cols_x, start, span, 0)
                sub_u = lax.dynamic_slice_in_dim(cols_u, start, span, 0)
                energy = kernel_tile(rows_x, sub_x)
                return carry + jnp.dot(energy, sub_u, preferred_element_type=jnp.float32), None

            total, unused = lax.scan(add_sub, total, jnp.arange(N_NARROW, dtype=jnp.int32))
        return (total * rows_a[:, None]).reshape(NB, P_SIZE, NPROBE).sum(axis=1)

    result = lax.map(one_group, jnp.arange(N_GROUP, dtype=jnp.int32))
    return result.reshape(NIMG, NPROBE)
```

```python
import functools
import math

import jax
import jax.numpy as jnp
from jax import lax
from jax.experimental import pallas as pl
from jax.experimental.pallas import tpu as pltpu
from jax.sharding import PartitionSpec as P

P_SIZE = 49
PV = 75
NPROBE = 16
LANES = 128
WIDE = P_SIZE * PV
PACKED = (WIDE + 1 + 2 * NPROBE + LANES - 1) // LANES * LANES
TAIL = WIDE // LANES * LANES
COUNT_AT = WIDE - TAIL
PROBE_AT = COUNT_AT + 1
COL_NORM = PV
ROW_NORM = PV + 3
U_AT = PV + 6
A_AT = U_AT + NPROBE
ROWS = 1024
COLS = 512
SCALE = 2.0 * math.log2(math.e) / (2.0 * PV)
NT = (((1,), (1,)), ((), ()))
NN = (((1,), (0,)), ((), ()))


def dot(a, b, dims=NN):
    return lax.dot_general(a, b, dims, preferred_element_type=jnp.float32)


def iota(shape, dim):
    return lax.broadcasted_iota(jnp.int32, shape, dim)


def parts(value):
    hi = value.astype(jnp.bfloat16).astype(jnp.float32)
    rest = value - hi
    mid = rest.astype(jnp.bfloat16).astype(jnp.float32)
    return hi, mid, (rest - mid).astype(jnp.bfloat16).astype(jnp.float32)


def order(tail):
    number = tail.shape[0]
    count = tail[:, COUNT_AT : COUNT_AT + 1]
    key = count * number + (number - 1 - iota((number, 1), 0)).astype(jnp.float32)
    square = (number, number)
    key_here = jnp.broadcast_to(key, square)
    key_along = jnp.sum(jnp.where(iota(square, 0) == iota(square, 1), key_here, 0.0), axis=0, keepdims=True)
    rank = jnp.sum((key_here > key_along).astype(jnp.float32), axis=0, keepdims=True)
    chosen = (iota(square, 0).astype(jnp.float32) == rank).astype(jnp.bfloat16)
    patch = iota((number, LANES), 1).astype(jnp.float32)
    valid = jnp.sum((count > patch).astype(jnp.float32), axis=0, keepdims=True)
    taken = ((valid.astype(jnp.int32) + 15) // 16 * 16).astype(jnp.float32)
    before = (iota((LANES, LANES), 0) < iota((LANES, LANES), 1)).astype(jnp.bfloat16)
    first = dot(jnp.broadcast_to(taken, (8, LANES)).astype(jnp.bfloat16), before)
    return chosen, first.astype(jnp.int32)


def spread(sorted_ref, weights_ref, first_ref, at, x_ref, is_rows, extra):
    number = sorted_ref.shape[0]
    shape = (number, LANES)
    lane = iota(shape, 1)
    tail = sorted_ref[:, TAIL : TAIL + LANES]
    count = tail[:, COUNT_AT : COUNT_AT + 1]
    if not is_rows:
        probe = tail[:, PROBE_AT : PROBE_AT + NPROBE] + tail[:, PROBE_AT + NPROBE : PROBE_AT + 2 * NPROBE]
        probe = jnp.concatenate(
            [jnp.zeros((number, U_AT), jnp.float32), probe, jnp.zeros((number, LANES - U_AT - NPROBE), jnp.float32)], axis=1
        )
    for p in range(P_SIZE):
        values = jnp.where(lane < PV, sorted_ref[:, p * PV : p * PV + LANES], 0.0)
        hi, mid, low = parts(-0.5 * jnp.sum(values * values, axis=1, keepdims=True))
        alpha = weights_ref[0, p] * (count > float(p)).astype(jnp.float32) / count
        mine, other = (ROW_NORM, COL_NORM) if is_rows else (COL_NORM, ROW_NORM)
        for step, part in enumerate((hi, mid, low)):
            values = jnp.where(lane == mine + step, part, values)
        values = jnp.where((lane >= other) & (lane < other + 3), 1.0, values)
        if is_rows:
            for step, part in enumerate(parts(alpha)):
                values = jnp.where(lane == A_AT + step, part, values)
        else:
            values = values + alpha * probe
        start = pl.multiple_of(first_ref[at, p], 16)
        x_ref[pl.ds(start, number), :] = values.astype(jnp.bfloat16)
        if is_rows:
            extra[0][pl.ds(start, number), :] = extra[1]
    total = pl.multiple_of(first_ref[at, P_SIZE], 16)
    size = ROWS if is_rows else COLS
    x_ref[pl.ds(total, size), :] = jnp.zeros((size, LANES), jnp.bfloat16)
    if is_rows:
        extra[0][pl.ds(total, size), :] = jnp.zeros((size, extra[0].shape[1]), jnp.bfloat16)
    return total


def energies(images, meetings, plan_ref, mine_ref, weights_ref, near_ref, far_ref, out_ref,
             row_sorted, col_sorted, row_x, col_x, owner, col_u, product, first_v, first_s, sem):
    mine = mine_ref[0]
    near = near_ref.shape[0]
    far = far_ref.shape[0]
    cols = images * meetings

    line = iota((cols, far), 0)
    source = jnp.zeros((cols, far), jnp.int32)
    for meeting in range(meetings):
        here = (line >= meeting * images) & (line < (meeting + 1) * images)
        source = jnp.where(here, plan_ref[meeting, mine] * images + line - meeting * images, source)
    met = (iota((cols, far), 1) == source).astype(jnp.bfloat16)

    row_order, row_first = order(near_ref[:, TAIL : TAIL + LANES].astype(jnp.float32))
    col_order, col_first = order(dot(met, far_ref[:, TAIL : TAIL + LANES]))
    first_v[0:8, :] = row_first
    first_v[8:16, :] = col_first
    copy = pltpu.make_async_copy(first_v, first_s, sem)
    copy.start()
    for target in (row_sorted, col_sorted):
        target[:, PACKED:] = jnp.zeros((target.shape[0], LANES), jnp.float32)
    row_sorted[:, 0:PACKED] = dot(row_order, near_ref[...])
    col_sorted[:, 0:PACKED] = dot(dot(col_order, met).astype(jnp.bfloat16), far_ref[...])
    copy.wait()
    col_total = spread(col_sorted, weights_ref, first_s, 8, col_x, False, None)
    row_total = spread(row_sorted, weights_ref, first_s, 0, row_x, True, (owner, row_order))

    col_steps = (col_total + COLS - 1) // COLS
    row_steps = (row_total + ROWS - 1) // ROWS
    pick_u = (iota((NPROBE, LANES), 1) == iota((NPROBE, LANES), 0) + U_AT).astype(jnp.bfloat16)
    at_a = iota((NPROBE, LANES), 1)
    pick_a = ((at_a >= A_AT) & (at_a < A_AT + 3)).astype(jnp.bfloat16)

    def turn(step, unused):
        here = pl.ds(pl.multiple_of(step * COLS, COLS), COLS)
        col_u[:, here] = dot(pick_u, col_x[here, :], NT).astype(jnp.bfloat16)
        return unused

    lax.fori_loop(0, col_steps, turn, 0)
    product[...] = jnp.zeros_like(product)

    def one_row(row, unused):
        rows = pl.ds(pl.multiple_of(row * ROWS, ROWS), ROWS)
        x_rows = row_x[rows, :]

        def one_col(col, total):
            here = pl.ds(pl.multiple_of(col * COLS, COLS), COLS)
            inner = dot(col_x[here, :], x_rows, NT)
            energy = jnp.exp2(inner * SCALE).astype(jnp.bfloat16)
            return total + dot(col_u[:, here], energy)

        total = lax.fori_loop(0, col_steps, one_col, jnp.zeros((NPROBE, ROWS), jnp.float32))
        weighted = jnp.concatenate(parts(total * dot(pick_a, x_rows, NT)), axis=0).astype(jnp.bfloat16)
        sums = dot(weighted, owner[rows, :])
        product[...] += sums[0:NPROBE] + sums[NPROBE : 2 * NPROBE] + sums[2 * NPROBE :]
        return unused

    lax.fori_loop(0, row_steps, one_row, 0)
    out_ref[...] = product[...].T


def local_terms(plan, mine, weights, near, far, images):
    meetings = plan.shape[0]
    rows, cols = near.shape[0], images * meetings
    vmem = pl.BlockSpec(memory_space=pltpu.VMEM)
    smem = pl.BlockSpec(memory_space=pltpu.SMEM)
    room = lambda number, size: (number * P_SIZE + 15) // size * size + size + number + size
    return pl.pallas_call(
        functools.partial(energies, images, meetings),
        out_shape=jax.ShapeDtypeStruct((rows, NPROBE), jnp.float32),
        in_specs=[smem, smem, smem, vmem, vmem],
        out_specs=vmem,
        scratch_shapes=[
            pltpu.VMEM((rows, PACKED + LANES), jnp.float32),
            pltpu.VMEM((cols, PACKED + LANES), jnp.float32),
            pltpu.VMEM((room(rows, ROWS), LANES), jnp.bfloat16),
            pltpu.VMEM((room(cols, COLS), LANES), jnp.bfloat16),
            pltpu.VMEM((room(rows, ROWS), rows), jnp.bfloat16),
            pltpu.VMEM((NPROBE, room(cols, COLS)), jnp.bfloat16),
            pltpu.VMEM((NPROBE, rows), jnp.float32),
            pltpu.VMEM((16, LANES), jnp.int32),
            pltpu.SMEM((16, LANES), jnp.int32),
            pltpu.SemaphoreType.DMA,
        ],
        compiler_params=pltpu.CompilerParams(vmem_limit_bytes=52 * 2**20),
        name="energies",
    )(plan, mine, weights, near, far)


def shards(patches, counts, weights, probes, plan):
    images = patches.shape[0]
    hi = lax.reduce_precision(probes, 8, 7)
    packed = jnp.concatenate(
        [
            patches,
            counts[:, None].astype(jnp.bfloat16),
            hi.astype(jnp.bfloat16),
            (probes - hi).astype(jnp.bfloat16),
            jnp.zeros((images, PACKED - WIDE - 1 - 2 * NPROBE), jnp.bfloat16),
        ],
        axis=1,
    )
    near = lax.all_gather(packed, "narrow", axis=0, tiled=True)
    far = lax.all_gather(packed, "group", axis=0, tiled=True)
    mine = lax.axis_index("group").reshape(1)
    terms = local_terms(plan, mine, weights[None, :], near, far, images)
    subs = lax.axis_size("narrow")
    me = lax.axis_index("narrow")
    pieces = terms.reshape(subs, images, NPROBE)
    total = lax.dynamic_index_in_dim(pieces, me, 0, keepdims=False)
    for step in range(1, subs):
        sent = lax.dynamic_index_in_dim(pieces, lax.rem(me + step, subs), 0, keepdims=False)
        total = total + lax.ppermute(sent, "narrow", [(i, (i + step) % subs) for i in range(subs)])
    return total


def solution(mesh):
    return jax.shard_map(
        shards,
        mesh=mesh,
        in_specs=(
            P(("group", "narrow"), None),
            P(("group", "narrow")),
            P(),
            P(("group", "narrow"), None),
            P(),
        ),
        out_specs=P(("group", "narrow"), None),
        check_vma=False,
    )
```

```python
import functools
import math

import jax
import jax.numpy as jnp
from jax import lax
from jax.experimental import pallas as pl
from jax.experimental.pallas import tpu as pltpu
from jax.sharding import PartitionSpec as P

P_SIZE = 49
PV = 75
NPROBE = 16
LANES = 128
NORM_AT = PV
ALPHA_AT = PV + 3
FEATURES = 5
STRIDE = PV + FEATURES
WIDE = P_SIZE * STRIDE
PACKED = (WIDE + 1 + 2 * NPROBE + LANES - 1) // LANES * LANES
TAIL = WIDE // LANES * LANES
COUNT_AT = WIDE - TAIL
PROBE_AT = COUNT_AT + 1
ROWS = 1024
COLS = 512
SCALE = 2.0 * math.log2(math.e) / (2.0 * PV)
NT = (((1,), (1,)), ((), ()))
NN = (((1,), (0,)), ((), ()))
VMEM = pl.BlockSpec(memory_space=pltpu.VMEM)
SMEM = pl.BlockSpec(memory_space=pltpu.SMEM)
ANY = pl.BlockSpec(memory_space=pl.ANY)


def dot(a, b, dims=NN):
    return lax.dot_general(a, b, dims, preferred_element_type=jnp.float32)


def iota(shape, dim):
    return lax.broadcasted_iota(jnp.int32, shape, dim)


def parts(value):
    hi = value.astype(jnp.bfloat16).astype(jnp.float32)
    rest = value - hi
    mid = rest.astype(jnp.bfloat16).astype(jnp.float32)
    return hi, mid, (rest - mid).astype(jnp.bfloat16).astype(jnp.float32)


def pack_kernel(patches_ref, counts_ref, weights_ref, probes_ref, out_ref):
    images, wide = patches_ref.shape
    shape = (images, LANES)
    lane = iota(shape, 1)
    square = (images, images)
    along = jnp.broadcast_to(counts_ref[...].astype(jnp.float32), square)
    count = jnp.sum(jnp.where(iota(square, 0) == iota(square, 1), along, 0.0), axis=1, keepdims=True)
    weight = jnp.concatenate([weights_ref[...], jnp.zeros((1, LANES - P_SIZE), jnp.float32)], axis=1)
    alpha = weight * (lane.astype(jnp.float32) < count).astype(jnp.float32) / count
    patches = []
    for p in range(P_SIZE):
        values = patches_ref[:, p * PV : min(p * PV + LANES, wide)]
        if values.shape[1] < LANES:
            values = jnp.concatenate([values, jnp.zeros((images, LANES - values.shape[1]), jnp.bfloat16)], axis=1)
        patches.append(jnp.where(lane < PV, values, jnp.bfloat16(0)))
    stacked = jnp.concatenate(patches, axis=0).astype(jnp.float32)
    squares = stacked * stacked
    ones = jnp.ones((LANES, LANES), jnp.bfloat16)
    high = squares.astype(jnp.bfloat16)
    norm = dot(high, ones) + dot((squares - high.astype(jnp.float32)).astype(jnp.bfloat16), ones)
    norms = [part.astype(jnp.bfloat16) for part in parts(-0.5 * norm)]
    alphas = [part.astype(jnp.bfloat16) for part in parts(alpha)[:2]]
    tiles = [None] * (PACKED // LANES)

    def put(values, start):
        tile, shift = divmod(start, LANES)
        moved = pltpu.roll(values, shift, 1) if shift else values
        first = jnp.where(lane >= shift, moved, jnp.bfloat16(0)) if shift else moved
        tiles[tile] = first if tiles[tile] is None else tiles[tile] + first
        if shift and tile + 1 < len(tiles):
            tiles[tile + 1] = jnp.where(lane < shift, moved, jnp.bfloat16(0))

    for p in range(P_SIZE):
        values = patches[p]
        for step, part in enumerate(norms):
            values = jnp.where(lane == NORM_AT + step, part[p * images : (p + 1) * images], values)
        for step, part in enumerate(alphas):
            values = jnp.where(lane == ALPHA_AT + step, pltpu.roll(part, (ALPHA_AT + step - p) % LANES, 1), values)
        put(values, p * STRIDE)
    probe_hi, probe_low, unused = parts(probes_ref[...])
    rest = jnp.concatenate(
        [count, probe_hi, probe_low, jnp.zeros((images, LANES - 1 - 2 * NPROBE), jnp.float32)], axis=1
    )
    put(rest.astype(jnp.bfloat16), WIDE)
    for tile, values in enumerate(tiles):
        out_ref[:, tile * LANES : (tile + 1) * LANES] = values


def pack(patches, counts, weights, probes):
    return pl.pallas_call(
        pack_kernel,
        out_shape=jax.ShapeDtypeStruct((patches.shape[0], PACKED), jnp.bfloat16),
        in_specs=[VMEM] * 4,
        out_specs=VMEM,
        name="pack",
    )(patches, counts[None, :], weights[None, :], probes)


def order(tail):
    number = tail.shape[0]
    count = tail[:, COUNT_AT : COUNT_AT + 1]
    key = count * number + (number - 1 - iota((number, 1), 0)).astype(jnp.float32)
    square = (number, number)
    key_here = jnp.broadcast_to(key, square)
    key_along = jnp.sum(jnp.where(iota(square, 0) == iota(square, 1), key_here, 0.0), axis=0, keepdims=True)
    rank = jnp.sum((key_here > key_along).astype(jnp.float32), axis=0, keepdims=True)
    chosen = (iota(square, 0).astype(jnp.float32) == rank).astype(jnp.bfloat16)
    patch = iota((number, LANES), 1).astype(jnp.float32)
    valid = jnp.sum((count > patch).astype(jnp.float32), axis=0, keepdims=True)
    taken = ((valid.astype(jnp.int32) + 15) // 16 * 16).astype(jnp.float32)
    before = (iota((LANES, LANES), 0) < iota((LANES, LANES), 1)).astype(jnp.bfloat16)
    first = dot(jnp.broadcast_to(taken, (8, LANES)).astype(jnp.bfloat16), before)
    return chosen, first.astype(jnp.int32)


def spread(sorted_ref, chosen, first_ref, at, x_ref, owner_ref, size):
    number = sorted_ref.shape[0]
    lane = iota((number, LANES), 1)
    for p in range(P_SIZE):
        values = jnp.where(lane < STRIDE, sorted_ref[:, p * STRIDE : p * STRIDE + LANES], jnp.bfloat16(0))
        start = pl.multiple_of(first_ref[at, p], 16)
        x_ref[pl.ds(start, number), :] = values
        owner_ref[pl.ds(start, number), :] = chosen
    total = pl.multiple_of(first_ref[at, P_SIZE], 16)
    x_ref[pl.ds(total, size), :] = jnp.zeros((size, LANES), jnp.bfloat16)
    owner_ref[pl.ds(total, size), :] = jnp.zeros((size, number), jnp.bfloat16)
    return (total + size - 1) // size


def energies(images, meetings, counted, *refs):
    near_number, far_number = counted
    plan_ref, mine_ref = refs[:2]
    near_parts = refs[2 : 2 + near_number]
    far_parts = refs[2 + near_number : 2 + near_number + far_number]
    (out_ref, near_ref, far_ref, row_sorted, col_sorted, row_x, col_x, row_owner, col_owner, col_u, product,
     first_v, first_s, sem, near_sem, far_sem) = refs[2 + near_number + far_number :]
    copies = []
    for target, sources, sems in ((far_ref, far_parts, far_sem), (near_ref, near_parts, near_sem)):
        at = 0
        for index, source in enumerate(sources):
            size = source.shape[0]
            copies.append(pltpu.make_async_copy(source, target.at[pl.ds(at, size), :], sems.at[index]))
            at += size
    for copy in copies:
        copy.start()

    mine = mine_ref[0]
    far = far_ref.shape[0]
    cols = images * meetings
    line = iota((cols, far), 0)
    source = jnp.zeros((cols, far), jnp.int32)
    for meeting in range(meetings):
        here = (line >= meeting * images) & (line < (meeting + 1) * images)
        apart = plan_ref[meeting, mine] ^ mine
        slot = (apart & 1) * (far // images // 2) + (apart >> 1)
        source = jnp.where(here, slot * images + line - meeting * images, source)
    met = (iota((cols, far), 1) == source).astype(jnp.bfloat16)
    for target in (row_sorted, col_sorted):
        target[:, PACKED:] = jnp.zeros((target.shape[0], LANES), jnp.bfloat16)
    for copy in copies:
        copy.wait()

    row_order, row_first = order(near_ref[:, TAIL : TAIL + LANES].astype(jnp.float32))
    col_tail = dot(met, far_ref[:, TAIL : TAIL + LANES])
    col_order, col_first = order(col_tail)
    first_v[0:8, :] = row_first
    first_v[8:16, :] = col_first
    copy = pltpu.make_async_copy(first_v, first_s, sem)
    copy.start()
    row_sorted[:, 0:PACKED] = dot(row_order, near_ref[...]).astype(jnp.bfloat16)
    col_sorted[:, 0:PACKED] = dot(dot(col_order, met).astype(jnp.bfloat16), far_ref[...]).astype(jnp.bfloat16)
    copy.wait()
    col_steps = spread(col_sorted, col_order, first_s, 8, col_x, col_owner, COLS)
    row_steps = spread(row_sorted, row_order, first_s, 0, row_x, row_owner, ROWS)

    pick = (NPROBE, LANES)
    pick_norm = ((iota(pick, 1) >= NORM_AT) & (iota(pick, 1) < ALPHA_AT)).astype(jnp.bfloat16)
    pick_alpha = ((iota(pick, 1) >= ALPHA_AT) & (iota(pick, 1) < STRIDE)).astype(jnp.bfloat16)
    both = (2 * NPROBE, LANES)
    pick_probe = (iota(both, 1) == iota(both, 0) + PROBE_AT).astype(jnp.bfloat16)
    probes = dot(pick_probe, col_tail.astype(jnp.bfloat16), NT).astype(jnp.bfloat16)

    def turn(step, unused):
        here = pl.ds(pl.multiple_of(step * COLS, COLS), COLS)
        mine = dot(probes, col_owner[here, :], NT)
        alpha = dot(pick_alpha, col_x[here, :], NT)
        col_u[:, here] = (alpha * (mine[:NPROBE] + mine[NPROBE:])).astype(jnp.bfloat16)
        return unused

    lax.fori_loop(0, col_steps, turn, 0)
    product[...] = jnp.zeros_like(product)
    row_lane = iota((ROWS, LANES), 1)

    def one_row(row, unused):
        rows = pl.ds(pl.multiple_of(row * ROWS, ROWS), ROWS)
        x_rows = row_x[rows, :]
        norm = dot(pick_norm, x_rows, NT)[0:1]
        alpha = dot(pick_alpha, x_rows, NT)
        x_rows = jnp.where(
            row_lane < NORM_AT, x_rows, jnp.where(row_lane < ALPHA_AT, jnp.bfloat16(1), jnp.bfloat16(0))
        )

        def one_col(col, total):
            here = pl.ds(pl.multiple_of(col * COLS, COLS), COLS)
            inner = dot(col_x[here, :], x_rows, NT)
            energy = jnp.exp2((inner + norm) * SCALE).astype(jnp.bfloat16)
            return total + dot(col_u[:, here], energy)

        total = lax.fori_loop(0, col_steps, one_col, jnp.zeros((NPROBE, ROWS), jnp.float32))
        weighted = jnp.concatenate(parts(total * alpha), axis=0).astype(jnp.bfloat16)
        sums = dot(weighted, row_owner[rows, :])
        product[...] += sums[0:NPROBE] + sums[NPROBE : 2 * NPROBE] + sums[2 * NPROBE :]
        return unused

    lax.fori_loop(0, row_steps, one_row, 0)
    out_ref[...] = product[...].T


def local_terms(plan, mine, near, far, images):
    meetings = plan.shape[0]
    rows, reach = sum(a.shape[0] for a in near), sum(a.shape[0] for a in far)
    cols = images * meetings
    room = lambda number, size: (number * P_SIZE + 15) // size * size + size + number + size
    return pl.pallas_call(
        functools.partial(energies, images, meetings, (len(near), len(far))),
        out_shape=jax.ShapeDtypeStruct((rows, NPROBE), jnp.float32),
        in_specs=[SMEM, SMEM] + [ANY] * (len(near) + len(far)),
        out_specs=VMEM,
        scratch_shapes=[
            pltpu.VMEM((rows, PACKED), jnp.bfloat16),
            pltpu.VMEM((reach, PACKED), jnp.bfloat16),
            pltpu.VMEM((rows, PACKED + LANES), jnp.bfloat16),
            pltpu.VMEM((cols, PACKED + LANES), jnp.bfloat16),
            pltpu.VMEM((room(rows, ROWS), LANES), jnp.bfloat16),
            pltpu.VMEM((room(cols, COLS), LANES), jnp.bfloat16),
            pltpu.VMEM((room(rows, ROWS), rows), jnp.bfloat16),
            pltpu.VMEM((room(cols, COLS), cols), jnp.bfloat16),
            pltpu.VMEM((NPROBE, room(cols, COLS)), jnp.bfloat16),
            pltpu.VMEM((NPROBE, rows), jnp.float32),
            pltpu.VMEM((16, LANES), jnp.int32),
            pltpu.SMEM((16, LANES), jnp.int32),
            pltpu.SemaphoreType.DMA,
            pltpu.SemaphoreType.DMA((len(near),)),
            pltpu.SemaphoreType.DMA((len(far),)),
        ],
        compiler_params=pltpu.CompilerParams(vmem_limit_bytes=52 * 2**20),
        name="energies",
    )(plan, mine, *near, *far)


def shards(patches, counts, weights, probes, plan):
    images = patches.shape[0]
    packed = pack(patches, counts, weights, probes)
    groups, subs = lax.axis_size("group"), lax.axis_size("narrow")

    def swap(array, apart):
        return lax.ppermute(array, "group", [(i, i ^ apart) for i in range(groups)])

    def turn(array, step):
        return lax.ppermute(array, "narrow", [(i, (i + step) % subs) for i in range(subs)])

    even = [packed] + [swap(packed, apart) for apart in range(2, groups, 2)]
    far = even + [swap(array, 1) for array in even]
    near = [packed] + [turn(packed, step) for step in range(1, subs)]
    mine = lax.axis_index("group").reshape(1)
    terms = local_terms(plan, mine, near, far, images)
    total = terms[:images]
    for step in range(1, subs):
        total = total + turn(terms[step * images : (step + 1) * images], -step)
    return total


def solution(mesh):
    return jax.shard_map(
        shards,
        mesh=mesh,
        in_specs=(
            P(("group", "narrow"), None),
            P(("group", "narrow")),
            P(),
            P(("group", "narrow"), None),
            P(),
        ),
        out_specs=P(("group", "narrow"), None),
        check_vma=False,
    )
```

```python
import functools
import math

import jax
import jax.numpy as jnp
from jax import lax
from jax.experimental import pallas as pl
from jax.experimental.pallas import tpu as pltpu
from jax.sharding import PartitionSpec as P

P_SIZE = 49
PV = 75
NPROBE = 16
LANES = 128
NORM_AT = PV
ALPHA_AT = PV + 3
FEATURES = 5
STRIDE = PV + FEATURES
WIDE = P_SIZE * STRIDE
PACKED = (WIDE + 1 + 2 * NPROBE + LANES - 1) // LANES * LANES
TAIL = WIDE // LANES * LANES
COUNT_AT = WIDE - TAIL
PROBE_AT = COUNT_AT + 1
OWNER_AT = STRIDE
ROWS = (1024, 256)
COLS = (1024, 256)
SCALE = 2.0 * math.log2(math.e) / (2.0 * PV)
NT = (((1,), (1,)), ((), ()))
NN = (((1,), (0,)), ((), ()))
VMEM = pl.BlockSpec(memory_space=pltpu.VMEM)
SMEM = pl.BlockSpec(memory_space=pltpu.SMEM)
HBM = pl.BlockSpec(memory_space=pltpu.HBM)


def dot(a, b, dims=NN):
    return lax.dot_general(a, b, dims, preferred_element_type=jnp.float32)


def iota(shape, dim):
    return lax.broadcasted_iota(jnp.int32, shape, dim)


def parts(value):
    hi = value.astype(jnp.bfloat16).astype(jnp.float32)
    rest = value - hi
    mid = rest.astype(jnp.bfloat16).astype(jnp.float32)
    return hi, mid, (rest - mid).astype(jnp.bfloat16).astype(jnp.float32)


def pack_kernel(mine_ref, *refs):
    sources, (out_ref, met_ref), targets, sem = refs[:5], refs[5:7], refs[7:12], refs[12]
    copies = [pltpu.make_async_copy(s, t, sem.at[k]) for k, (s, t) in enumerate(zip(sources, targets))]
    for copy in copies:
        copy.start()
    for copy in copies:
        copy.wait()
    patches_ref, counts_ref, weights_ref, probes_ref, plan_ref = targets
    images, wide = patches_ref.shape
    cols, far = met_ref.shape
    plan = plan_ref[...]
    mine = mine_ref[0]
    partner = jnp.sum(jnp.where(iota(plan.shape, 1) == mine, plan, 0), axis=1, keepdims=True)
    line = iota((cols, far), 0)
    source = jnp.zeros((cols, far), jnp.int32)
    for meeting in range(plan.shape[0]):
        here = (line >= meeting * images) & (line < (meeting + 1) * images)
        apart = partner[meeting : meeting + 1, :] ^ mine
        slot = (apart & 1) * (far // images // 2) + (apart >> 1)
        source = jnp.where(here, slot * images + line - meeting * images, source)
    met_ref[...] = (iota((cols, far), 1) == source).astype(jnp.bfloat16)

    shape = (images, LANES)
    lane = iota(shape, 1)
    square = (images, images)
    along = jnp.broadcast_to(counts_ref[...].astype(jnp.float32), square)
    count = jnp.sum(jnp.where(iota(square, 0) == iota(square, 1), along, 0.0), axis=1, keepdims=True)
    weight = jnp.concatenate([weights_ref[...], jnp.zeros((1, LANES - P_SIZE), jnp.float32)], axis=1)
    alpha = weight * (lane.astype(jnp.float32) < count).astype(jnp.float32) / count
    patches = []
    for p in range(P_SIZE):
        values = patches_ref[:, p * PV : min(p * PV + LANES, wide)]
        if values.shape[1] < LANES:
            values = jnp.concatenate([values, jnp.zeros((images, LANES - values.shape[1]), jnp.bfloat16)], axis=1)
        patches.append(jnp.where(lane < PV, values, jnp.bfloat16(0)))
    stacked = jnp.concatenate(patches, axis=0).astype(jnp.float32)
    squares = stacked * stacked
    ones = jnp.ones((LANES, LANES), jnp.bfloat16)
    high = squares.astype(jnp.bfloat16)
    norm = dot(high, ones) + dot((squares - high.astype(jnp.float32)).astype(jnp.bfloat16), ones)
    norms = [part.astype(jnp.bfloat16) for part in parts(-0.5 * norm)]
    alphas = [part.astype(jnp.bfloat16) for part in parts(alpha)[:2]]
    tiles = [None] * (PACKED // LANES)

    def put(values, start):
        tile, shift = divmod(start, LANES)
        moved = pltpu.roll(values, shift, 1) if shift else values
        first = jnp.where(lane >= shift, moved, jnp.bfloat16(0)) if shift else moved
        tiles[tile] = first if tiles[tile] is None else tiles[tile] + first
        if shift and tile + 1 < len(tiles):
            tiles[tile + 1] = jnp.where(lane < shift, moved, jnp.bfloat16(0))

    for p in range(P_SIZE):
        values = patches[p]
        for step, part in enumerate(norms):
            values = jnp.where(lane == NORM_AT + step, part[p * images : (p + 1) * images], values)
        for step, part in enumerate(alphas):
            values = jnp.where(lane == ALPHA_AT + step, pltpu.roll(part, (ALPHA_AT + step - p) % LANES, 1), values)
        put(values, p * STRIDE)
    probe_hi, probe_low, unused = parts(probes_ref[...])
    rest = jnp.concatenate(
        [count, probe_hi, probe_low, jnp.zeros((images, LANES - 1 - 2 * NPROBE), jnp.float32)], axis=1
    )
    put(rest.astype(jnp.bfloat16), WIDE)
    for tile, values in enumerate(tiles):
        out_ref[:, tile * LANES : (tile + 1) * LANES] = values


def pack(patches, counts, weights, probes, plan, mine):
    images = patches.shape[0]
    given = (patches, counts[None, :], weights[None, :], probes, plan)
    return pl.pallas_call(
        pack_kernel,
        out_shape=(
            jax.ShapeDtypeStruct((images, PACKED), jnp.bfloat16),
            jax.ShapeDtypeStruct((images * plan.shape[0], images * plan.shape[1]), jnp.bfloat16),
        ),
        in_specs=[SMEM] + [HBM] * len(given),
        out_specs=(VMEM, VMEM),
        scratch_shapes=[pltpu.VMEM(a.shape, a.dtype) for a in given] + [pltpu.SemaphoreType.DMA((len(given),))],
        compiler_params=pltpu.CompilerParams(vmem_limit_bytes=8 * 2**20),
        name="pack",
    )(mine, *given)


def order(tail):
    number = tail.shape[0]
    count = tail[:, COUNT_AT : COUNT_AT + 1]
    key = count * number + (number - 1 - iota((number, 1), 0)).astype(jnp.float32)
    square = (number, number)
    key_here = jnp.broadcast_to(key, square)
    key_along = jnp.sum(jnp.where(iota(square, 0) == iota(square, 1), key_here, 0.0), axis=0, keepdims=True)
    rank = jnp.sum((key_here > key_along).astype(jnp.float32), axis=0, keepdims=True)
    chosen = (iota(square, 0).astype(jnp.float32) == rank).astype(jnp.bfloat16)
    patch = iota((number, LANES), 1).astype(jnp.float32)
    valid = jnp.sum((count > patch).astype(jnp.float32), axis=0, keepdims=True)
    before = (iota((LANES, LANES), 0) < iota((LANES, LANES), 1)).astype(jnp.bfloat16)
    first = dot(jnp.broadcast_to(valid, (8, LANES)).astype(jnp.bfloat16), before)
    return chosen, first.astype(jnp.int32)


def spread(sorted_ref, chosen, first_ref, at, x_ref, room):
    number = sorted_ref.shape[0]
    lane = iota((number, LANES), 1)
    owner = jnp.sum(jnp.where(chosen > 0, iota((number, number), 1).astype(jnp.float32), 0.0), axis=1, keepdims=True)
    owner = jnp.where(lane == OWNER_AT, owner, 0.0)
    for p in range(P_SIZE):
        values = jnp.where(lane < STRIDE, sorted_ref[:, p * STRIDE : p * STRIDE + LANES], owner)
        x_ref[pl.ds(first_ref[at, p], number), :] = values
    total = first_ref[at, P_SIZE]
    x_ref[pl.ds(total, room), :] = jnp.zeros((room, LANES), jnp.float32)
    return total


def cover(total, sizes, step, carry):
    large, small = sizes
    number = (total + large - small) // large
    carry = lax.fori_loop(0, number, lambda k, c: step(pl.multiple_of(k * large, large), large, c), carry)
    rest = (total - number * large + small - 1) // small
    start = pl.multiple_of(number * large, large)
    return lax.fori_loop(0, rest, lambda k, c: step(start, small, c), carry)


def rank_kernel(*refs):
    chosen_ref, first_ref = refs[-2:]
    tail = jnp.concatenate([part[:, TAIL : TAIL + LANES] for part in refs[:-2]], axis=0)
    chosen, first = order(tail.astype(jnp.float32))
    chosen_ref[...] = chosen
    first_ref[...] = first


def rank(near):
    images = sum(a.shape[0] for a in near)
    return pl.pallas_call(
        rank_kernel,
        out_shape=(jax.ShapeDtypeStruct((images, images), jnp.bfloat16), jax.ShapeDtypeStruct((8, LANES), jnp.int32)),
        in_specs=[VMEM] * len(near),
        out_specs=(VMEM, VMEM),
        compiler_params=pltpu.CompilerParams(vmem_limit_bytes=8 * 2**20),
        cost_estimate=pl.CostEstimate(flops=2 * 10**10, bytes_accessed=10**6, transcendentals=0),
        name="rank",
    )(*near)


def energies(counted, *refs):
    near_number, far_number = counted
    row_first, row_order, met_ref = refs[:3]
    near_parts = refs[3 : 3 + near_number]
    far_parts = refs[3 + near_number : 3 + near_number + far_number]
    (out_ref, row_sorted, col_sorted, row_x, col_f, col_x, col_u, product, first_v, first_s, sem) = refs[
        3 + near_number + far_number :
    ]
    cols = met_ref.shape[0]
    met = met_ref[...]
    for target in (row_sorted, col_sorted):
        target[:, PACKED:] = jnp.zeros((target.shape[0], LANES), jnp.float32)
    tails = jnp.concatenate([part[:, TAIL : TAIL + LANES] for part in far_parts], axis=0)
    col_tail = dot(met, tails)
    col_order, col_first = order(col_tail)
    first_v[...] = col_first
    copy = pltpu.make_async_copy(first_v, first_s, sem)
    copy.start()
    row_sorted[:, 0:PACKED] = dot(row_order[...], jnp.concatenate([part[...] for part in near_parts], axis=0))
    col_chosen = dot(col_order, met).astype(jnp.bfloat16)
    col_sorted[:, 0:PACKED] = dot(col_chosen, jnp.concatenate([part[...] for part in far_parts], axis=0))
    row_total = spread(row_sorted, row_order[...], row_first, 0, row_x, ROWS[0])
    copy.wait()
    col_total = spread(col_sorted, col_order, first_s, 0, col_f, COLS[0])

    line, lane = iota((NPROBE, LANES), 0), iota((NPROBE, LANES), 1)
    pick = (
        ((line == 0) & (lane >= NORM_AT) & (lane < ALPHA_AT))
        | ((line == 1) & (lane >= ALPHA_AT) & (lane < STRIDE))
        | ((line == 2) & (lane == OWNER_AT))
    ).astype(jnp.bfloat16)
    both = (2 * NPROBE, LANES)
    pick_probe = (iota(both, 1) == iota(both, 0) + PROBE_AT).astype(jnp.bfloat16)
    probes = dot(pick_probe, col_tail.astype(jnp.bfloat16), NT).astype(jnp.bfloat16)

    def owned(picked, number, size):
        return (iota((number, size), 0).astype(jnp.float32) == picked[2:3]).astype(jnp.bfloat16)

    def prepare(start, size, unused):
        here = pl.ds(start, size)
        x_cols = col_f[here, :].astype(jnp.bfloat16)
        col_x[here, :] = x_cols
        picked = dot(pick, x_cols, NT)
        mine = dot(probes, owned(picked, cols, size))
        col_u[:, here] = (picked[1:2] * (mine[:NPROBE] + mine[NPROBE:])).astype(jnp.bfloat16)
        return unused

    cover(col_total, COLS, prepare, 0)
    product[...] = jnp.zeros_like(product)

    def one_row(start, size, unused):
        x_rows = row_x[pl.ds(start, size), :].astype(jnp.bfloat16)
        picked = dot(pick, x_rows, NT)
        row_lane = iota((size, LANES), 1)
        x_rows = jnp.where(
            row_lane < NORM_AT, x_rows, jnp.where(row_lane < ALPHA_AT, jnp.bfloat16(1), jnp.bfloat16(0))
        )

        def one_col(start, size, total):
            here = pl.ds(start, size)
            inner = dot(col_x[here, :], x_rows, NT)
            energy = jnp.exp2((inner + picked[0:1]) * SCALE).astype(jnp.bfloat16)
            return total + dot(col_u[:, here], energy)

        total = cover(col_total, COLS, one_col, jnp.zeros((NPROBE, size), jnp.float32))
        weighted = jnp.concatenate(parts(total * picked[1:2]), axis=0).astype(jnp.bfloat16)
        sums = dot(weighted, owned(picked, product.shape[1], size), NT)
        product[...] += sums[0:NPROBE] + sums[NPROBE : 2 * NPROBE] + sums[2 * NPROBE :]
        return unused

    cover(row_total, ROWS, one_row, 0)
    out_ref[...] = product[...].T


def local_terms(met, ranked, near, far):
    row_order, row_first = ranked
    rows, cols = row_order.shape[0], met.shape[0]
    row_room = rows * P_SIZE + rows + ROWS[0]
    col_room = (cols * P_SIZE + cols) // COLS[0] * COLS[0] + 2 * COLS[0]
    return pl.pallas_call(
        functools.partial(energies, (len(near), len(far))),
        out_shape=jax.ShapeDtypeStruct((rows, NPROBE), jnp.float32),
        in_specs=[SMEM] + [VMEM] * (2 + len(near) + len(far)),
        out_specs=VMEM,
        scratch_shapes=[
            pltpu.VMEM((rows, PACKED + LANES), jnp.float32),
            pltpu.VMEM((cols, PACKED + LANES), jnp.float32),
            pltpu.VMEM((row_room, LANES), jnp.float32),
            pltpu.VMEM((col_room, LANES), jnp.float32),
            pltpu.VMEM((col_room, LANES), jnp.bfloat16),
            pltpu.VMEM((NPROBE, col_room), jnp.bfloat16),
            pltpu.VMEM((NPROBE, rows), jnp.float32),
            pltpu.VMEM((8, LANES), jnp.int32),
            pltpu.SMEM((8, LANES), jnp.int32),
            pltpu.SemaphoreType.DMA,
        ],
        compiler_params=pltpu.CompilerParams(vmem_limit_bytes=40 * 2**20),
        name="energies",
    )(row_first, row_order, met, *near, *far)


def shards(patches, counts, weights, probes, plan):
    images = patches.shape[0]
    mine = lax.axis_index("group").reshape(1)
    packed, met = pack(patches, counts, weights, probes, plan, mine)
    groups, subs = lax.axis_size("group"), lax.axis_size("narrow")

    def swap(array, apart):
        return lax.ppermute(array, "group", [(i, i ^ apart) for i in range(groups)])

    def across(array, apart):
        return lax.ppermute(array, "narrow", [(i, i ^ apart) for i in range(subs)])

    even = [packed] + [swap(packed, apart) for apart in range(2, groups, 2)]
    far = even + [swap(array, 1) for array in even]
    near = [packed]
    for apart in range(1, subs):
        low = apart & -apart
        near.append(across(near[apart - low], low))
    terms = local_terms(met, rank(near), near, far)
    total = terms[:images]
    for apart in range(1, subs):
        total = total + across(terms[apart * images : (apart + 1) * images], apart)
    return total


def solution(mesh):
    return jax.shard_map(
        shards,
        mesh=mesh,
        in_specs=(
            P(("group", "narrow"), None),
            P(("group", "narrow")),
            P(),
            P(("group", "narrow"), None),
            P(),
        ),
        out_specs=P(("group", "narrow"), None),
        check_vma=False,
    )
```

```python
import functools
import math

import jax
import jax.numpy as jnp
from jax import lax
from jax.experimental import pallas as pl
from jax.experimental.pallas import tpu as pltpu
from jax.sharding import PartitionSpec as P

P_SIZE = 49
PV = 75
NPROBE = 16
LANES = 128
NORM_AT = PV
ALPHA_AT = PV + 3
FEATURES = 5
STRIDE = PV + FEATURES
WIDE = P_SIZE * STRIDE
PACKED = (WIDE + 1 + 2 * NPROBE + LANES - 1) // LANES * LANES
TAIL = WIDE // LANES * LANES
COUNT_AT = WIDE - TAIL
PROBE_AT = COUNT_AT + 1
OWNER_AT = STRIDE
ROWS = (896, 1024, 256)
COLS = (896, 1024, 256)
PREPARED = (2048, 2048, 256)
SCALE = 2.0 * math.log2(math.e) / (2.0 * PV)
NT = (((1,), (1,)), ((), ()))
NN = (((1,), (0,)), ((), ()))
VMEM = pl.BlockSpec(memory_space=pltpu.VMEM)
SMEM = pl.BlockSpec(memory_space=pltpu.SMEM)
HBM = pl.BlockSpec(memory_space=pltpu.HBM)


def dot(a, b, dims=NN):
    return lax.dot_general(a, b, dims, preferred_element_type=jnp.float32)


def iota(shape, dim):
    return lax.broadcasted_iota(jnp.int32, shape, dim)


def parts(value):
    hi = value.astype(jnp.bfloat16).astype(jnp.float32)
    rest = value - hi
    mid = rest.astype(jnp.bfloat16).astype(jnp.float32)
    return hi, mid, (rest - mid).astype(jnp.bfloat16).astype(jnp.float32)


def pack_kernel(mine_ref, *refs):
    sources, (out_ref, met_ref), targets, sem = refs[:5], refs[5:7], refs[7:12], refs[12]
    copies = [pltpu.make_async_copy(s, t, sem.at[k]) for k, (s, t) in enumerate(zip(sources, targets))]
    for copy in copies:
        copy.start()
    for copy in copies:
        copy.wait()
    patches_ref, counts_ref, weights_ref, probes_ref, plan_ref = targets
    images, wide = patches_ref.shape
    cols, far = met_ref.shape
    plan = plan_ref[...]
    mine = mine_ref[0]
    partner = jnp.sum(jnp.where(iota(plan.shape, 1) == mine, plan, 0), axis=1, keepdims=True)
    line = iota((cols, far), 0)
    source = jnp.zeros((cols, far), jnp.int32)
    for meeting in range(plan.shape[0]):
        here = (line >= meeting * images) & (line < (meeting + 1) * images)
        apart = partner[meeting : meeting + 1, :] ^ mine
        slot = (apart & 1) * (far // images // 2) + (apart >> 1)
        source = jnp.where(here, slot * images + line - meeting * images, source)
    met_ref[...] = (iota((cols, far), 1) == source).astype(jnp.bfloat16)

    shape = (images, LANES)
    lane = iota(shape, 1)
    square = (images, images)
    along = jnp.broadcast_to(counts_ref[...].astype(jnp.float32), square)
    count = jnp.sum(jnp.where(iota(square, 0) == iota(square, 1), along, 0.0), axis=1, keepdims=True)
    weight = jnp.concatenate([weights_ref[...], jnp.zeros((1, LANES - P_SIZE), jnp.float32)], axis=1)
    alpha = weight * (lane.astype(jnp.float32) < count).astype(jnp.float32) / count
    patches = []
    for p in range(P_SIZE):
        values = patches_ref[:, p * PV : min(p * PV + LANES, wide)]
        if values.shape[1] < LANES:
            values = jnp.concatenate([values, jnp.zeros((images, LANES - values.shape[1]), jnp.bfloat16)], axis=1)
        patches.append(jnp.where(lane < PV, values, jnp.bfloat16(0)))
    stacked = jnp.concatenate(patches, axis=0).astype(jnp.float32)
    squares = stacked * stacked
    ones = jnp.ones((LANES, LANES), jnp.bfloat16)
    high = squares.astype(jnp.bfloat16)
    norm = dot(high, ones) + dot((squares - high.astype(jnp.float32)).astype(jnp.bfloat16), ones)
    norms = [part.astype(jnp.bfloat16) for part in parts(-0.5 * norm)]
    alphas = [part.astype(jnp.bfloat16) for part in parts(alpha)[:2]]
    tiles = [None] * (PACKED // LANES)

    def put(values, start):
        tile, shift = divmod(start, LANES)
        moved = pltpu.roll(values, shift, 1) if shift else values
        first = jnp.where(lane >= shift, moved, jnp.bfloat16(0)) if shift else moved
        tiles[tile] = first if tiles[tile] is None else tiles[tile] + first
        if shift and tile + 1 < len(tiles):
            tiles[tile + 1] = jnp.where(lane < shift, moved, jnp.bfloat16(0))

    for p in range(P_SIZE):
        values = patches[p]
        for step, part in enumerate(norms):
            values = jnp.where(lane == NORM_AT + step, part[p * images : (p + 1) * images], values)
        for step, part in enumerate(alphas):
            values = jnp.where(lane == ALPHA_AT + step, pltpu.roll(part, (ALPHA_AT + step - p) % LANES, 1), values)
        put(values, p * STRIDE)
    probe_hi, probe_low, unused = parts(probes_ref[...])
    rest = jnp.concatenate(
        [count, probe_hi, probe_low, jnp.zeros((images, LANES - 1 - 2 * NPROBE), jnp.float32)], axis=1
    )
    put(rest.astype(jnp.bfloat16), WIDE)
    for tile, values in enumerate(tiles):
        out_ref[:, tile * LANES : (tile + 1) * LANES] = values


def pack(patches, counts, weights, probes, plan, mine):
    images = patches.shape[0]
    given = (patches, counts[None, :], weights[None, :], probes, plan)
    return pl.pallas_call(
        pack_kernel,
        out_shape=(
            jax.ShapeDtypeStruct((images, PACKED), jnp.bfloat16),
            jax.ShapeDtypeStruct((images * plan.shape[0], images * plan.shape[1]), jnp.bfloat16),
        ),
        in_specs=[SMEM] + [HBM] * len(given),
        out_specs=(VMEM, VMEM),
        scratch_shapes=[pltpu.VMEM(a.shape, a.dtype) for a in given] + [pltpu.SemaphoreType.DMA((len(given),))],
        compiler_params=pltpu.CompilerParams(vmem_limit_bytes=8 * 2**20),
        name="pack",
    )(mine, *given)


def order(tail):
    number = tail.shape[0]
    count = tail[:, COUNT_AT : COUNT_AT + 1]
    key = count * number + (number - 1 - iota((number, 1), 0)).astype(jnp.float32)
    square = (number, number)
    key_here = jnp.broadcast_to(key, square)
    key_along = jnp.sum(jnp.where(iota(square, 0) == iota(square, 1), key_here, 0.0), axis=0, keepdims=True)
    rank = jnp.sum((key_here > key_along).astype(jnp.float32), axis=0, keepdims=True)
    chosen = (iota(square, 0).astype(jnp.float32) == rank).astype(jnp.bfloat16)
    patch = iota((number, LANES), 1).astype(jnp.float32)
    valid = jnp.sum((count > patch).astype(jnp.float32), axis=0, keepdims=True)
    before = (iota((LANES, LANES), 0) < iota((LANES, LANES), 1)).astype(jnp.bfloat16)
    first = dot(jnp.broadcast_to(valid, (8, LANES)).astype(jnp.bfloat16), before)
    return chosen, first.astype(jnp.int32)


def owners(chosen):
    number = chosen.shape[0]
    owner = jnp.sum(jnp.where(chosen > 0, iota((number, number), 1).astype(jnp.float32), 0.0), axis=1, keepdims=True)
    return jnp.where(iota((number, LANES), 1) == OWNER_AT, owner, 0.0)


def spread(sorted_ref, owner, first_ref, x_ref, room):
    number = sorted_ref.shape[0]
    lane = iota((number, LANES), 1)
    for p in range(P_SIZE):
        values = jnp.where(lane < STRIDE, sorted_ref[:, p * STRIDE : p * STRIDE + LANES], owner)
        x_ref[pl.ds(first_ref[0, p], number), :] = values
    total = first_ref[0, P_SIZE]
    x_ref[pl.ds(total, room), :] = jnp.zeros((room, LANES), jnp.float32)
    return total


def cover(total, sizes, step, carry):
    tight, large, small = sizes
    fits = total <= 2 * tight

    def run(number, size, base, carry):
        return lax.fori_loop(0, number, lambda k, c: step(pl.multiple_of(base + k * size, LANES), size, c), carry)

    carry = run(jnp.where(fits, (total + tight - 1) // tight, 0), tight, 0, carry)
    number = jnp.where(fits, 0, (total + large - small) // large)
    carry = run(number, large, 0, carry)
    rest = jnp.where(fits, 0, (total - number * large + small - 1) // small)
    return run(rest, small, number * large, carry)


def rank_rows_kernel(*refs):
    which_ref, owner_ref, first_ref = refs[-3:]
    tail = jnp.concatenate([part[:, TAIL : TAIL + LANES] for part in refs[:-3]], axis=0)
    which_ref[...], first_ref[...] = order(tail.astype(jnp.float32))
    owner_ref[...] = owners(which_ref[...])


def rank_cols_kernel(met_ref, *refs):
    which_ref, owner_ref, first_ref, probe_ref = refs[-4:]
    met = met_ref[...]
    tail = dot(met, jnp.concatenate([part[:, TAIL : TAIL + LANES] for part in refs[:-4]], axis=0))
    chosen, first_ref[...] = order(tail)
    which_ref[...] = dot(chosen, met).astype(jnp.bfloat16)
    owner_ref[...] = owners(chosen)
    both = (2 * NPROBE, LANES)
    pick_probe = (iota(both, 1) == iota(both, 0) + PROBE_AT).astype(jnp.bfloat16)
    probe_ref[...] = dot(pick_probe, tail.astype(jnp.bfloat16), NT).astype(jnp.bfloat16)


def rank(kernel, number, given, extra, flops):
    return pl.pallas_call(
        kernel,
        out_shape=(
            jax.ShapeDtypeStruct((number, sum(a.shape[0] for a in given[-extra:])), jnp.bfloat16),
            jax.ShapeDtypeStruct((number, LANES), jnp.float32),
            jax.ShapeDtypeStruct((8, LANES), jnp.int32),
        )
        + ((jax.ShapeDtypeStruct((2 * NPROBE, number), jnp.bfloat16),) if extra < len(given) else ()),
        in_specs=[VMEM] * len(given),
        out_specs=(VMEM,) * (3 if extra == len(given) else 4),
        compiler_params=pltpu.CompilerParams(vmem_limit_bytes=8 * 2**20),
        cost_estimate=pl.CostEstimate(flops=flops, bytes_accessed=10**6, transcendentals=0),
        name="rank",
    )(*given)


def energies(counted, *refs):
    near_number, far_number = counted
    row_given, col_given, row_which, row_owner, col_which, col_owner, probe_ref = refs[:7]
    near_parts = refs[7 : 7 + near_number]
    far_parts = refs[7 + near_number : 7 + near_number + far_number]
    (out_ref, row_sorted, col_sorted, row_x, col_f, col_x, col_u, product, row_first, col_first, sem) = refs[
        7 + near_number + far_number :
    ]
    cols = col_owner.shape[0]
    copies = [pltpu.make_async_copy(s, t, sem.at[k]) for k, (s, t) in enumerate(((col_given, col_first), (row_given, row_first)))]
    for copy in copies:
        copy.start()
    product[...] = jnp.zeros_like(product)
    col_sorted[...] = dot(col_which[...], jnp.concatenate([part[...] for part in far_parts], axis=0))
    row_sorted[...] = dot(row_which[...], jnp.concatenate([part[...] for part in near_parts], axis=0))
    copies[0].wait()
    col_total = spread(col_sorted, col_owner[...], col_first, col_f, COLS[1])
    copies[1].wait()
    row_total = spread(row_sorted, row_owner[...], row_first, row_x, ROWS[1])
    probes = probe_ref[...]

    line, lane = iota((NPROBE, LANES), 0), iota((NPROBE, LANES), 1)
    pick = (
        ((line == 0) & (lane >= NORM_AT) & (lane < ALPHA_AT))
        | ((line == 1) & (lane >= ALPHA_AT) & (lane < STRIDE))
        | ((line == 2) & (lane == OWNER_AT))
    ).astype(jnp.bfloat16)
    def owned(picked, number, size):
        return (iota((number, size), 0).astype(jnp.float32) == picked[2:3]).astype(jnp.bfloat16)

    def prepare(start, size, unused):
        here = pl.ds(start, size)
        x_cols = col_f[here, :].astype(jnp.bfloat16)
        col_x[here, :] = x_cols
        picked = dot(pick, x_cols, NT)
        mine = dot(probes, owned(picked, cols, size))
        col_u[:, here] = (picked[1:2] * (mine[:NPROBE] + mine[NPROBE:])).astype(jnp.bfloat16)
        return unused

    cover(col_total, PREPARED, prepare, 0)

    def one_row(start, size, unused):
        x_rows = row_x[pl.ds(start, size), :].astype(jnp.bfloat16)
        picked = dot(pick, x_rows, NT)
        row_lane = iota((size, LANES), 1)
        x_rows = jnp.where(
            row_lane < NORM_AT, x_rows, jnp.where(row_lane < ALPHA_AT, jnp.bfloat16(1), jnp.bfloat16(0))
        )

        def one_col(start, size, total):
            here = pl.ds(start, size)
            inner = dot(col_x[here, :], x_rows, NT)
            energy = jnp.exp2((inner + picked[0:1]) * SCALE).astype(jnp.bfloat16)
            return total + dot(col_u[:, here], energy)

        total = cover(col_total, COLS, one_col, jnp.zeros((NPROBE, size), jnp.float32))
        weighted = jnp.concatenate(parts(total * picked[1:2]), axis=0).astype(jnp.bfloat16)
        sums = dot(weighted, owned(picked, product.shape[1], size), NT)
        product[...] += sums[0:NPROBE] + sums[NPROBE : 2 * NPROBE] + sums[2 * NPROBE :]
        return unused

    cover(row_total, ROWS, one_row, 0)
    out_ref[...] = product[...].T


def local_terms(rows_rank, cols_rank, near, far):
    row_which, row_owner, row_first = rows_rank
    col_which, col_owner, col_first, probes = cols_rank
    rows, cols = row_owner.shape[0], col_owner.shape[0]
    row_room = rows * P_SIZE + rows + ROWS[1]
    col_room = (cols * P_SIZE + cols) // COLS[1] * COLS[1] + COLS[1] + PREPARED[1]
    return pl.pallas_call(
        functools.partial(energies, (len(near), len(far))),
        out_shape=jax.ShapeDtypeStruct((rows, NPROBE), jnp.float32),
        in_specs=[VMEM] * (7 + len(near) + len(far)),
        out_specs=VMEM,
        scratch_shapes=[
            pltpu.VMEM((rows, PACKED), jnp.float32),
            pltpu.VMEM((cols, PACKED), jnp.float32),
            pltpu.VMEM((row_room, LANES), jnp.float32),
            pltpu.VMEM((col_room, LANES), jnp.float32),
            pltpu.VMEM((col_room, LANES), jnp.bfloat16),
            pltpu.VMEM((NPROBE, col_room), jnp.bfloat16),
            pltpu.VMEM((NPROBE, rows), jnp.float32),
            pltpu.SMEM((8, LANES), jnp.int32),
            pltpu.SMEM((8, LANES), jnp.int32),
            pltpu.SemaphoreType.DMA((2,)),
        ],
        compiler_params=pltpu.CompilerParams(vmem_limit_bytes=40 * 2**20),
        name="energies",
    )(row_first, col_first, row_which, row_owner, col_which, col_owner, probes, *near, *far)


def shards(patches, counts, weights, probes, plan):
    images = patches.shape[0]
    mine = lax.axis_index("group").reshape(1)
    packed, met = pack(patches, counts, weights, probes, plan, mine)
    groups, subs = lax.axis_size("group"), lax.axis_size("narrow")

    def swap(array, apart):
        return lax.ppermute(array, "group", [(i, i ^ apart) for i in range(groups)])

    def across(array, apart):
        return lax.ppermute(array, "narrow", [(i, i ^ apart) for i in range(subs)])

    even = [packed] + [swap(packed, apart) for apart in range(2, groups, 2)]
    far = even + [swap(array, 1) for array in even]
    near = [packed]
    for apart in range(1, subs):
        low = apart & -apart
        near.append(across(near[apart - low], low))
    rows_rank = rank(rank_rows_kernel, subs * images, near, subs, 20 * 10**9)
    cols_rank = rank(rank_cols_kernel, met.shape[0], [met, *far], groups, 2 * 10**9)
    terms = local_terms(rows_rank, cols_rank, near, far)
    total = terms[:images]
    for apart in range(subs - 1, 0, -1):
        total = total + across(terms[apart * images : (apart + 1) * images], apart)
    return total


def solution(mesh):
    return jax.shard_map(
        shards,
        mesh=mesh,
        in_specs=(
            P(("group", "narrow"), None),
            P(("group", "narrow")),
            P(),
            P(("group", "narrow"), None),
            P(),
        ),
        out_specs=P(("group", "narrow"), None),
        check_vma=False,
    )
```

```python
import functools
import math

import jax
import jax.numpy as jnp
from jax import lax
from jax.experimental import pallas as pl
from jax.experimental.pallas import tpu as pltpu
from jax.sharding import PartitionSpec as P

P_SIZE = 49
PV = 75
NPROBE = 16
LANES = 128
NORM_AT = PV
ALPHA_AT = PV + 3
FEATURES = 5
STRIDE = PV + FEATURES
WIDE = P_SIZE * STRIDE
PACKED = (WIDE + 1 + 2 * NPROBE + LANES - 1) // LANES * LANES
TAIL = WIDE // LANES * LANES
COUNT_AT = WIDE - TAIL
PROBE_AT = COUNT_AT + 1
OWNER_AT = STRIDE
ROWS = ((1792, 1), (2048, 1), (1024, None))
COLS = ((896, 2), (1024, None))
PREPARED = ((2048, None),)
FILL = 256
SCALE = 2.0 * math.log2(math.e) / (2.0 * PV)
NT = (((1,), (1,)), ((), ()))
NN = (((1,), (0,)), ((), ()))
VMEM = pl.BlockSpec(memory_space=pltpu.VMEM)
SMEM = pl.BlockSpec(memory_space=pltpu.SMEM)


def dot(a, b, dims=NN):
    return lax.dot_general(a, b, dims, preferred_element_type=jnp.float32)


def iota(shape, dim):
    return lax.broadcasted_iota(jnp.int32, shape, dim)


def parts(value):
    hi = value.astype(jnp.bfloat16).astype(jnp.float32)
    rest = value - hi
    mid = rest.astype(jnp.bfloat16).astype(jnp.float32)
    return hi, mid, (rest - mid).astype(jnp.bfloat16).astype(jnp.float32)


def pack_kernel(mine_ref, *refs):
    patches_ref, counts_ref, weights_ref, probes_ref, plan_ref, out_ref, met_ref = refs
    images, wide = patches_ref.shape
    cols, far = met_ref.shape
    plan = plan_ref[...]
    mine = mine_ref[0]
    partner = jnp.sum(jnp.where(iota(plan.shape, 1) == mine, plan, 0), axis=1, keepdims=True)
    line = iota((cols, far), 0)
    source = jnp.zeros((cols, far), jnp.int32)
    for meeting in range(plan.shape[0]):
        here = (line >= meeting * images) & (line < (meeting + 1) * images)
        apart = partner[meeting : meeting + 1, :] ^ mine
        slot = (apart & 1) * (far // images // 2) + (apart >> 1)
        source = jnp.where(here, slot * images + line - meeting * images, source)
    met_ref[...] = (iota((cols, far), 1) == source).astype(jnp.bfloat16)

    shape = (images, LANES)
    lane = iota(shape, 1)
    square = (images, images)
    along = jnp.broadcast_to(counts_ref[...].astype(jnp.float32), square)
    count = jnp.sum(jnp.where(iota(square, 0) == iota(square, 1), along, 0.0), axis=1, keepdims=True)
    weight = jnp.concatenate([weights_ref[...], jnp.zeros((1, LANES - P_SIZE), jnp.float32)], axis=1)
    alpha = weight * (lane.astype(jnp.float32) < count).astype(jnp.float32) / count
    patches = []
    for p in range(P_SIZE):
        values = patches_ref[:, p * PV : min(p * PV + LANES, wide)]
        if values.shape[1] < LANES:
            values = jnp.concatenate([values, jnp.zeros((images, LANES - values.shape[1]), jnp.bfloat16)], axis=1)
        patches.append(jnp.where(lane < PV, values, jnp.bfloat16(0)))
    stacked = jnp.concatenate(patches, axis=0).astype(jnp.float32)
    squares = stacked * stacked
    ones = jnp.ones((LANES, LANES), jnp.bfloat16)
    high = squares.astype(jnp.bfloat16)
    norm = dot(high, ones) + dot((squares - high.astype(jnp.float32)).astype(jnp.bfloat16), ones)
    norms = [part.astype(jnp.bfloat16) for part in parts(-0.5 * norm)]
    alphas = [part.astype(jnp.bfloat16) for part in parts(alpha)[:2]]
    tiles = [None] * (PACKED // LANES)

    def put(values, start):
        tile, shift = divmod(start, LANES)
        moved = pltpu.roll(values, shift, 1) if shift else values
        first = jnp.where(lane >= shift, moved, jnp.bfloat16(0)) if shift else moved
        tiles[tile] = first if tiles[tile] is None else tiles[tile] + first
        if shift and tile + 1 < len(tiles):
            tiles[tile + 1] = jnp.where(lane < shift, moved, jnp.bfloat16(0))

    for p in range(P_SIZE):
        values = patches[p]
        for step, part in enumerate(norms):
            values = jnp.where(lane == NORM_AT + step, part[p * images : (p + 1) * images], values)
        for step, part in enumerate(alphas):
            values = jnp.where(lane == ALPHA_AT + step, pltpu.roll(part, (ALPHA_AT + step - p) % LANES, 1), values)
        put(values, p * STRIDE)
    probe_hi, probe_low, unused = parts(probes_ref[...])
    rest = jnp.concatenate(
        [count, probe_hi, probe_low, jnp.zeros((images, LANES - 1 - 2 * NPROBE), jnp.float32)], axis=1
    )
    put(rest.astype(jnp.bfloat16), WIDE)
    for tile, values in enumerate(tiles):
        out_ref[:, tile * LANES : (tile + 1) * LANES] = values


def pack(patches, counts, weights, probes, plan, mine):
    images = patches.shape[0]
    given = (patches, counts[None, :], weights[None, :], probes, plan)
    return pl.pallas_call(
        pack_kernel,
        out_shape=(
            jax.ShapeDtypeStruct((images, PACKED), jnp.bfloat16),
            jax.ShapeDtypeStruct((images * plan.shape[0], images * plan.shape[1]), jnp.bfloat16),
        ),
        in_specs=[SMEM] + [VMEM] * len(given),
        out_specs=(VMEM, VMEM),
        compiler_params=pltpu.CompilerParams(vmem_limit_bytes=8 * 2**20),
        name="pack",
    )(mine, *given)


def order(tail):
    number = tail.shape[0]
    count = tail[:, COUNT_AT : COUNT_AT + 1]
    key = count * number + (number - 1 - iota((number, 1), 0)).astype(jnp.float32)
    square = (number, number)
    key_here = jnp.broadcast_to(key, square)
    key_along = jnp.sum(jnp.where(iota(square, 0) == iota(square, 1), key_here, 0.0), axis=0, keepdims=True)
    rank = jnp.sum((key_here > key_along).astype(jnp.float32), axis=0, keepdims=True)
    chosen = (iota(square, 0).astype(jnp.float32) == rank).astype(jnp.bfloat16)
    patch = iota((number, LANES), 1).astype(jnp.float32)
    valid = jnp.sum((count > patch).astype(jnp.float32), axis=0, keepdims=True)
    before = (iota((LANES, LANES), 0) < iota((LANES, LANES), 1)).astype(jnp.bfloat16)
    first = dot(jnp.broadcast_to(valid, (8, LANES)).astype(jnp.bfloat16), before)
    return chosen, first.astype(jnp.int32)


def owners(chosen):
    number = chosen.shape[0]
    owner = jnp.sum(jnp.where(chosen > 0, iota((number, number), 1).astype(jnp.float32), 0.0), axis=1, keepdims=True)
    return jnp.where(iota((number, LANES), 1) == OWNER_AT, owner, 0.0)


def spread(sorted_ref, owner, first_ref, x_ref, options):
    number = sorted_ref.shape[0]
    lane = iota((number, LANES), 1)
    for p in range(P_SIZE):
        values = jnp.where(lane < STRIDE, sorted_ref[:, p * STRIDE : p * STRIDE + LANES], owner)
        x_ref[pl.ds(first_ref[0, p], number), :] = values
    total = first_ref[0, P_SIZE]
    counts = choose(total, options)
    end = sum(count * size for count, (size, unused) in zip(counts, options))

    def clear(step, unused):
        x_ref[pl.ds(total + step * FILL, FILL), :] = jnp.zeros((FILL, LANES), jnp.float32)
        return unused

    lax.fori_loop(0, (end - total + FILL - 1) // FILL, clear, 0)
    return total, counts


def choose(total, options):
    counts, left = [], 1
    for size, most in options:
        need = (total + size - 1) // size
        fits = left if most is None else jnp.where(need <= most, left, 0)
        counts.append(fits * need)
        left = left - fits
    return counts


def cover(counts, options, step, carry):
    for count, (size, unused) in zip(counts, options):
        carry = lax.fori_loop(0, count, lambda k, c, size=size: step(pl.multiple_of(k * size, LANES), size, c), carry)
    return carry


def rank_rows_kernel(*refs):
    which_ref, owner_ref, first_ref = refs[-3:]
    tail = jnp.concatenate([part[:, TAIL : TAIL + LANES] for part in refs[:-3]], axis=0)
    which_ref[...], first_ref[...] = order(tail.astype(jnp.float32))
    owner_ref[...] = owners(which_ref[...])


def rank_cols_kernel(met_ref, *refs):
    which_ref, owner_ref, first_ref, probe_ref = refs[-4:]
    met = met_ref[...]
    tail = dot(met, jnp.concatenate([part[:, TAIL : TAIL + LANES] for part in refs[:-4]], axis=0))
    chosen, first_ref[...] = order(tail)
    which_ref[...] = dot(chosen, met).astype(jnp.bfloat16)
    owner_ref[...] = owners(chosen)
    both = (2 * NPROBE, LANES)
    pick_probe = (iota(both, 1) == iota(both, 0) + PROBE_AT).astype(jnp.bfloat16)
    probe_ref[...] = dot(pick_probe, tail.astype(jnp.bfloat16), NT).astype(jnp.bfloat16)


def rank(kernel, number, given, extra, flops):
    return pl.pallas_call(
        kernel,
        out_shape=(
            jax.ShapeDtypeStruct((number, sum(a.shape[0] for a in given[-extra:])), jnp.bfloat16),
            jax.ShapeDtypeStruct((number, LANES), jnp.float32),
            jax.ShapeDtypeStruct((8, LANES), jnp.int32),
        )
        + ((jax.ShapeDtypeStruct((2 * NPROBE, number), jnp.bfloat16),) if extra < len(given) else ()),
        in_specs=[VMEM] * len(given),
        out_specs=(VMEM,) * (3 if extra == len(given) else 4),
        compiler_params=pltpu.CompilerParams(vmem_limit_bytes=8 * 2**20),
        cost_estimate=pl.CostEstimate(flops=flops, bytes_accessed=10**6, transcendentals=0),
        name="rank",
    )(*given)


def energies(counted, *refs):
    near_number, far_number = counted
    row_given, col_given, row_which, row_owner, col_which, col_owner, probe_ref = refs[:7]
    near_parts = refs[7 : 7 + near_number]
    far_parts = refs[7 + near_number : 7 + near_number + far_number]
    (out_ref, row_sorted, col_sorted, row_x, col_f, col_x, col_u, product, row_first, col_first, sem) = refs[
        7 + near_number + far_number :
    ]
    cols = col_owner.shape[0]
    copies = [pltpu.make_async_copy(s, t, sem.at[k]) for k, (s, t) in enumerate(((col_given, col_first), (row_given, row_first)))]
    for copy in copies:
        copy.start()
    product[...] = jnp.zeros_like(product)
    col_sorted[...] = dot(col_which[...], jnp.concatenate([part[...] for part in far_parts], axis=0))
    row_sorted[...] = dot(row_which[...], jnp.concatenate([part[...] for part in near_parts], axis=0))
    copies[0].wait()
    col_total, col_counts = spread(col_sorted, col_owner[...], col_first, col_f, COLS)
    copies[1].wait()
    row_total, row_counts = spread(row_sorted, row_owner[...], row_first, row_x, ROWS)
    probes = probe_ref[...]

    line, lane = iota((NPROBE, LANES), 0), iota((NPROBE, LANES), 1)
    pick = (
        ((line == 0) & (lane >= NORM_AT) & (lane < ALPHA_AT))
        | ((line == 1) & (lane >= ALPHA_AT) & (lane < STRIDE))
        | ((line == 2) & (lane == OWNER_AT))
    ).astype(jnp.bfloat16)
    def owned(picked, number, size):
        return (iota((number, size), 0).astype(jnp.float32) == picked[2:3]).astype(jnp.bfloat16)

    def prepare(start, size, unused):
        here = pl.ds(start, size)
        x_cols = col_f[here, :].astype(jnp.bfloat16)
        col_x[here, :] = x_cols
        picked = dot(pick, x_cols, NT)
        mine = dot(probes, owned(picked, cols, size))
        col_u[:, here] = (picked[1:2] * (mine[:NPROBE] + mine[NPROBE:])).astype(jnp.bfloat16)
        return unused

    cover(choose(col_total, PREPARED), PREPARED, prepare, 0)

    def one_row(start, size, unused):
        x_rows = row_x[pl.ds(start, size), :].astype(jnp.bfloat16)
        picked = dot(pick, x_rows, NT)
        row_lane = iota((size, LANES), 1)
        x_rows = jnp.where(
            row_lane < NORM_AT, x_rows, jnp.where(row_lane < ALPHA_AT, jnp.bfloat16(1), jnp.bfloat16(0))
        )

        def one_col(start, size, total):
            here = pl.ds(start, size)
            inner = dot(col_x[here, :], x_rows, NT)
            energy = jnp.exp2((inner + picked[0:1]) * SCALE).astype(jnp.bfloat16)
            return total + dot(col_u[:, here], energy)

        total = cover(col_counts, COLS, one_col, jnp.zeros((NPROBE, size), jnp.float32))
        weighted = jnp.concatenate(parts(total * picked[1:2]), axis=0).astype(jnp.bfloat16)
        sums = dot(weighted, owned(picked, product.shape[1], size), NT)
        product[...] += sums[0:NPROBE] + sums[NPROBE : 2 * NPROBE] + sums[2 * NPROBE :]
        return unused

    cover(row_counts, ROWS, one_row, 0)
    out_ref[...] = product[...].T


def local_terms(rows_rank, cols_rank, near, far):
    row_which, row_owner, row_first = rows_rank
    col_which, col_owner, col_first, probes = cols_rank
    rows, cols = row_owner.shape[0], col_owner.shape[0]
    row_room = rows * P_SIZE + ROWS[1][0] + FILL
    col_room = (cols * P_SIZE // PREPARED[0][0] + 1) * PREPARED[0][0] + FILL
    return pl.pallas_call(
        functools.partial(energies, (len(near), len(far))),
        out_shape=jax.ShapeDtypeStruct((rows, NPROBE), jnp.float32),
        in_specs=[VMEM] * (7 + len(near) + len(far)),
        out_specs=VMEM,
        scratch_shapes=[
            pltpu.VMEM((rows, PACKED), jnp.float32),
            pltpu.VMEM((cols, PACKED), jnp.float32),
            pltpu.VMEM((row_room, LANES), jnp.float32),
            pltpu.VMEM((col_room, LANES), jnp.float32),
            pltpu.VMEM((col_room, LANES), jnp.bfloat16),
            pltpu.VMEM((NPROBE, col_room), jnp.bfloat16),
            pltpu.VMEM((NPROBE, rows), jnp.float32),
            pltpu.SMEM((8, LANES), jnp.int32),
            pltpu.SMEM((8, LANES), jnp.int32),
            pltpu.SemaphoreType.DMA((2,)),
        ],
        compiler_params=pltpu.CompilerParams(vmem_limit_bytes=40 * 2**20),
        name="energies",
    )(row_first, col_first, row_which, row_owner, col_which, col_owner, probes, *near, *far)


def shards(patches, counts, weights, probes, plan):
    images = patches.shape[0]
    mine = lax.axis_index("group").reshape(1)
    packed, met = pack(patches, counts, weights, probes, plan, mine)
    groups, subs = lax.axis_size("group"), lax.axis_size("narrow")

    def swap(array, apart):
        return lax.ppermute(array, "group", [(i, i ^ apart) for i in range(groups)])

    def across(array, apart):
        return lax.ppermute(array, "narrow", [(i, i ^ apart) for i in range(subs)])

    even = [packed] + [swap(packed, apart) for apart in range(groups - 2, 0, -2)][::-1]
    far = even + [swap(array, 1) for array in even]
    near = [packed]
    for apart in range(1, subs):
        low = apart & -apart
        near.append(across(near[apart - low], low))
    rows_rank = rank(rank_rows_kernel, subs * images, near, subs, 20 * 10**9)
    cols_rank = rank(rank_cols_kernel, met.shape[0], [met, *far], groups, 2 * 10**9)
    terms = local_terms(rows_rank, cols_rank, near, far)
    total = terms[:images]
    for apart in range(subs - 1, 0, -1):
        total = total + across(terms[apart * images : (apart + 1) * images], apart)
    return total


def solution(mesh):
    return jax.shard_map(
        shards,
        mesh=mesh,
        in_specs=(
            P(("group", "narrow"), None),
            P(("group", "narrow")),
            P(),
            P(("group", "narrow"), None),
            P(),
        ),
        out_specs=P(("group", "narrow"), None),
        check_vma=False,
    )
```

```python
import functools
import math

import jax
import jax.numpy as jnp
from jax import lax
from jax.experimental import pallas as pl
from jax.experimental.pallas import tpu as pltpu
from jax.sharding import PartitionSpec as P

P_SIZE = 49
PV = 75
NPROBE = 16
LANES = 128
NORM_AT = PV
ALPHA_AT = PV + 3
FEATURES = 5
STRIDE = PV + FEATURES
WIDE = P_SIZE * STRIDE
PACKED = (WIDE + 1 + 2 * NPROBE + LANES - 1) // LANES * LANES
TAIL = WIDE // LANES * LANES
COUNT_AT = WIDE - TAIL
PROBE_AT = COUNT_AT + 1
OWNER_AT = STRIDE
ROWS = ((1792, 1), (2048, 1), (1024, None))
COLS = ((896, 2), (1024, None))
PREPARED = ((2048, None),)
FILL = 256
SCALE = 2.0 * math.log2(math.e) / (2.0 * PV)
NT = (((1,), (1,)), ((), ()))
NN = (((1,), (0,)), ((), ()))
VMEM = pl.BlockSpec(memory_space=pltpu.VMEM)
SMEM = pl.BlockSpec(memory_space=pltpu.SMEM)


def dot(a, b, dims=NN):
    return lax.dot_general(a, b, dims, preferred_element_type=jnp.float32)


def iota(shape, dim):
    return lax.broadcasted_iota(jnp.int32, shape, dim)


def parts(value):
    hi = value.astype(jnp.bfloat16).astype(jnp.float32)
    rest = value - hi
    mid = rest.astype(jnp.bfloat16).astype(jnp.float32)
    return hi, mid, (rest - mid).astype(jnp.bfloat16).astype(jnp.float32)


def pack_kernel(mine_ref, *refs):
    patches_ref, counts_ref, weights_ref, probes_ref, plan_ref, out_ref, met_ref = refs
    images, wide = patches_ref.shape
    cols, far = met_ref.shape
    plan = plan_ref[...]
    mine = mine_ref[0]
    partner = jnp.sum(jnp.where(iota(plan.shape, 1) == mine, plan, 0), axis=1, keepdims=True)
    line = iota((cols, far), 0)
    source = jnp.zeros((cols, far), jnp.int32)
    for meeting in range(plan.shape[0]):
        here = (line >= meeting * images) & (line < (meeting + 1) * images)
        apart = partner[meeting : meeting + 1, :] ^ mine
        slot = (apart & 1) * (far // images // 2) + (apart >> 1)
        source = jnp.where(here, slot * images + line - meeting * images, source)
    met_ref[...] = (iota((cols, far), 1) == source).astype(jnp.bfloat16)

    shape = (images, LANES)
    lane = iota(shape, 1)
    square = (images, images)
    along = jnp.broadcast_to(counts_ref[...].astype(jnp.float32), square)
    count = jnp.sum(jnp.where(iota(square, 0) == iota(square, 1), along, 0.0), axis=1, keepdims=True)
    weight = jnp.concatenate([weights_ref[...], jnp.zeros((1, LANES - P_SIZE), jnp.float32)], axis=1)
    alpha = weight * (lane.astype(jnp.float32) < count).astype(jnp.float32) / count
    patches = []
    for p in range(P_SIZE):
        values = patches_ref[:, p * PV : min(p * PV + LANES, wide)]
        if values.shape[1] < LANES:
            values = jnp.concatenate([values, jnp.zeros((images, LANES - values.shape[1]), jnp.bfloat16)], axis=1)
        patches.append(jnp.where(lane < PV, values, jnp.bfloat16(0)))
    stacked = jnp.concatenate(patches, axis=0).astype(jnp.float32)
    squares = stacked * stacked
    ones = jnp.ones((LANES, LANES), jnp.bfloat16)
    high = squares.astype(jnp.bfloat16)
    norm = dot(high, ones) + dot((squares - high.astype(jnp.float32)).astype(jnp.bfloat16), ones)
    norms = [part.astype(jnp.bfloat16) for part in parts(-0.5 * norm)]
    alphas = [part.astype(jnp.bfloat16) for part in parts(alpha)[:2]]
    tiles = [None] * (PACKED // LANES)

    def put(values, start):
        tile, shift = divmod(start, LANES)
        moved = pltpu.roll(values, shift, 1) if shift else values
        first = jnp.where(lane >= shift, moved, jnp.bfloat16(0)) if shift else moved
        tiles[tile] = first if tiles[tile] is None else tiles[tile] + first
        if shift and tile + 1 < len(tiles):
            tiles[tile + 1] = jnp.where(lane < shift, moved, jnp.bfloat16(0))

    for p in range(P_SIZE):
        values = patches[p]
        for step, part in enumerate(norms):
            values = jnp.where(lane == NORM_AT + step, part[p * images : (p + 1) * images], values)
        for step, part in enumerate(alphas):
            values = jnp.where(lane == ALPHA_AT + step, pltpu.roll(part, (ALPHA_AT + step - p) % LANES, 1), values)
        put(values, p * STRIDE)
    probe_hi, probe_low, unused = parts(probes_ref[...])
    rest = jnp.concatenate(
        [count, probe_hi, probe_low, jnp.zeros((images, LANES - 1 - 2 * NPROBE), jnp.float32)], axis=1
    )
    put(rest.astype(jnp.bfloat16), WIDE)
    for tile, values in enumerate(tiles):
        out_ref[:, tile * LANES : (tile + 1) * LANES] = values


def pack(patches, counts, weights, probes, plan, mine):
    images = patches.shape[0]
    given = (patches, counts[None, :], weights[None, :], probes, plan)
    return pl.pallas_call(
        pack_kernel,
        out_shape=(
            jax.ShapeDtypeStruct((images, PACKED), jnp.bfloat16),
            jax.ShapeDtypeStruct((images * plan.shape[0], images * plan.shape[1]), jnp.bfloat16),
        ),
        in_specs=[SMEM] + [VMEM] * len(given),
        out_specs=(VMEM, VMEM),
        compiler_params=pltpu.CompilerParams(vmem_limit_bytes=8 * 2**20),
        name="pack",
    )(mine, *given)


def order(tail):
    number = tail.shape[0]
    count = tail[:, COUNT_AT : COUNT_AT + 1]
    key = count * number + (number - 1 - iota((number, 1), 0)).astype(jnp.float32)
    square = (number, number)
    key_here = jnp.broadcast_to(key, square)
    key_along = jnp.sum(jnp.where(iota(square, 0) == iota(square, 1), key_here, 0.0), axis=0, keepdims=True)
    rank = jnp.sum((key_here > key_along).astype(jnp.float32), axis=0, keepdims=True)
    chosen = (iota(square, 0).astype(jnp.float32) == rank).astype(jnp.bfloat16)
    patch = iota((number, LANES), 1).astype(jnp.float32)
    valid = jnp.sum((count > patch).astype(jnp.float32), axis=0, keepdims=True)
    before = (iota((LANES, LANES), 0) < iota((LANES, LANES), 1)).astype(jnp.bfloat16)
    first = dot(jnp.broadcast_to(valid, (8, LANES)).astype(jnp.bfloat16), before)
    return chosen, first.astype(jnp.int32)


def owners(chosen):
    number = chosen.shape[0]
    owner = jnp.sum(jnp.where(chosen > 0, iota((number, number), 1).astype(jnp.float32), 0.0), axis=1, keepdims=True)
    return jnp.where(iota((number, LANES), 1) == OWNER_AT, owner, 0.0)


def spread(sorted_ref, owner, first_ref, x_ref, options):
    number = sorted_ref.shape[0]
    lane = iota((number, LANES), 1)
    for p in range(P_SIZE):
        values = jnp.where(lane < STRIDE, sorted_ref[:, p * STRIDE : p * STRIDE + LANES].astype(jnp.float32), owner)
        x_ref[pl.ds(first_ref[0, p], number), :] = values
    total = first_ref[0, P_SIZE]
    counts = choose(total, options)
    end = sum(count * size for count, (size, unused) in zip(counts, options))

    def clear(step, unused):
        x_ref[pl.ds(total + step * FILL, FILL), :] = jnp.zeros((FILL, LANES), jnp.float32)
        return unused

    lax.fori_loop(0, (end - total + FILL - 1) // FILL, clear, 0)
    return total, counts


def choose(total, options):
    counts, left = [], 1
    for size, most in options:
        need = (total + size - 1) // size
        fits = left if most is None else jnp.where(need <= most, left, 0)
        counts.append(fits * need)
        left = left - fits
    return counts


def cover(counts, options, step, carry):
    for count, (size, unused) in zip(counts, options):
        carry = lax.fori_loop(0, count, lambda k, c, size=size: step(pl.multiple_of(k * size, LANES), size, c), carry)
    return carry


def rank_rows_kernel(*refs):
    which_ref, owner_ref, first_ref = refs[-3:]
    tail = jnp.concatenate([part[:, TAIL : TAIL + LANES] for part in refs[:-3]], axis=0)
    which_ref[...], first_ref[...] = order(tail.astype(jnp.float32))
    owner_ref[...] = owners(which_ref[...])


def rank_cols_kernel(met_ref, *refs):
    which_ref, owner_ref, first_ref, probe_ref = refs[-4:]
    met = met_ref[...]
    tail = dot(met, jnp.concatenate([part[:, TAIL : TAIL + LANES] for part in refs[:-4]], axis=0))
    chosen, first_ref[...] = order(tail)
    which_ref[...] = dot(chosen, met).astype(jnp.bfloat16)
    owner_ref[...] = owners(chosen)
    both = (2 * NPROBE, LANES)
    pick_probe = (iota(both, 1) == iota(both, 0) + PROBE_AT).astype(jnp.bfloat16)
    probe_ref[...] = dot(pick_probe, tail.astype(jnp.bfloat16), NT).astype(jnp.bfloat16)


def rank(kernel, number, given, extra, flops):
    return pl.pallas_call(
        kernel,
        out_shape=(
            jax.ShapeDtypeStruct((number, sum(a.shape[0] for a in given[-extra:])), jnp.bfloat16),
            jax.ShapeDtypeStruct((number, LANES), jnp.float32),
            jax.ShapeDtypeStruct((8, LANES), jnp.int32),
        )
        + ((jax.ShapeDtypeStruct((2 * NPROBE, number), jnp.bfloat16),) if extra < len(given) else ()),
        in_specs=[VMEM] * len(given),
        out_specs=(VMEM,) * (3 if extra == len(given) else 4),
        compiler_params=pltpu.CompilerParams(vmem_limit_bytes=8 * 2**20),
        cost_estimate=pl.CostEstimate(flops=flops, bytes_accessed=10**6, transcendentals=0),
        name="rank",
    )(*given)


def energies(counted, *refs):
    near_number, far_number = counted
    row_given, col_given, row_which, row_owner, col_which, col_owner, probe_ref = refs[:7]
    near_parts = refs[7 : 7 + near_number]
    far_parts = refs[7 + near_number : 7 + near_number + far_number]
    (out_ref, row_sorted, col_sorted, row_x, col_f, col_x, col_u, product, row_first, col_first, sem) = refs[
        7 + near_number + far_number :
    ]
    cols = col_owner.shape[0]
    copies = [pltpu.make_async_copy(s, t, sem.at[k]) for k, (s, t) in enumerate(((col_given, col_first), (row_given, row_first)))]
    for copy in copies:
        copy.start()
    product[...] = jnp.zeros_like(product)
    col_sorted[...] = dot(col_which[...], jnp.concatenate([part[...] for part in far_parts], axis=0)).astype(jnp.bfloat16)
    row_sorted[...] = dot(row_which[...], jnp.concatenate([part[...] for part in near_parts], axis=0)).astype(jnp.bfloat16)
    copies[0].wait()
    col_total, col_counts = spread(col_sorted, col_owner[...], col_first, col_f, COLS)
    copies[1].wait()
    row_total, row_counts = spread(row_sorted, row_owner[...], row_first, row_x, ROWS)
    probes = probe_ref[...]

    line, lane = iota((NPROBE, LANES), 0), iota((NPROBE, LANES), 1)
    pick = (
        ((line == 0) & (lane >= NORM_AT) & (lane < ALPHA_AT))
        | ((line == 1) & (lane >= ALPHA_AT) & (lane < STRIDE))
        | ((line == 2) & (lane == OWNER_AT))
    ).astype(jnp.bfloat16)
    def owned(picked, number, size):
        return (iota((number, size), 0).astype(jnp.float32) == picked[2:3]).astype(jnp.bfloat16)

    def prepare(start, size, unused):
        here = pl.ds(start, size)
        x_cols = col_f[here, :].astype(jnp.bfloat16)
        col_x[here, :] = x_cols
        picked = dot(pick, x_cols, NT)
        mine = dot(probes, owned(picked, cols, size))
        col_u[:, here] = (picked[1:2] * (mine[:NPROBE] + mine[NPROBE:])).astype(jnp.bfloat16)
        return unused

    cover(choose(col_total, PREPARED), PREPARED, prepare, 0)

    def one_row(start, size, unused):
        x_rows = row_x[pl.ds(start, size), :].astype(jnp.bfloat16)
        picked = dot(pick, x_rows, NT)
        row_lane = iota((size, LANES), 1)
        x_rows = jnp.where(
            row_lane < NORM_AT, x_rows, jnp.where(row_lane < ALPHA_AT, jnp.bfloat16(1), jnp.bfloat16(0))
        )

        def one_col(start, size, total):
            here = pl.ds(start, size)
            inner = dot(col_x[here, :], x_rows, NT)
            energy = jnp.exp2((inner + picked[0:1]) * SCALE).astype(jnp.bfloat16)
            return total + dot(col_u[:, here], energy)

        total = cover(col_counts, COLS, one_col, jnp.zeros((NPROBE, size), jnp.float32))
        weighted = jnp.concatenate(parts(total * picked[1:2]), axis=0).astype(jnp.bfloat16)
        sums = dot(weighted, owned(picked, product.shape[1], size), NT)
        product[...] += sums[0:NPROBE] + sums[NPROBE : 2 * NPROBE] + sums[2 * NPROBE :]
        return unused

    cover(row_counts, ROWS, one_row, 0)
    out_ref[...] = product[...].T


def local_terms(rows_rank, cols_rank, near, far):
    row_which, row_owner, row_first = rows_rank
    col_which, col_owner, col_first, probes = cols_rank
    rows, cols = row_owner.shape[0], col_owner.shape[0]
    row_room = rows * P_SIZE + ROWS[1][0] + FILL
    col_room = (cols * P_SIZE // PREPARED[0][0] + 1) * PREPARED[0][0] + FILL
    return pl.pallas_call(
        functools.partial(energies, (len(near), len(far))),
        out_shape=jax.ShapeDtypeStruct((rows, NPROBE), jnp.float32),
        in_specs=[VMEM] * (7 + len(near) + len(far)),
        out_specs=VMEM,
        scratch_shapes=[
            pltpu.VMEM((rows, PACKED), jnp.bfloat16),
            pltpu.VMEM((cols, PACKED), jnp.bfloat16),
            pltpu.VMEM((row_room, LANES), jnp.float32),
            pltpu.VMEM((col_room, LANES), jnp.float32),
            pltpu.VMEM((col_room, LANES), jnp.bfloat16),
            pltpu.VMEM((NPROBE, col_room), jnp.bfloat16),
            pltpu.VMEM((NPROBE, rows), jnp.float32),
            pltpu.SMEM((8, LANES), jnp.int32),
            pltpu.SMEM((8, LANES), jnp.int32),
            pltpu.SemaphoreType.DMA((2,)),
        ],
        compiler_params=pltpu.CompilerParams(vmem_limit_bytes=40 * 2**20),
        name="energies",
    )(row_first, col_first, row_which, row_owner, col_which, col_owner, probes, *near, *far)


def shards(patches, counts, weights, probes, plan):
    images = patches.shape[0]
    mine = lax.axis_index("group").reshape(1)
    packed, met = pack(patches, counts, weights, probes, plan, mine)
    groups, subs = lax.axis_size("group"), lax.axis_size("narrow")

    def swap(array, apart):
        return lax.ppermute(array, "group", [(i, i ^ apart) for i in range(groups)])

    def across(array, apart):
        return lax.ppermute(array, "narrow", [(i, i ^ apart) for i in range(subs)])

    even = [packed] + [swap(packed, apart) for apart in range(groups - 2, 0, -2)][::-1]
    far = even + [swap(array, 1) for array in even]
    near = [packed]
    for apart in range(1, subs):
        low = apart & -apart
        near.append(across(near[apart - low], low))
    rows_rank = rank(rank_rows_kernel, subs * images, near, subs, 20 * 10**9)
    cols_rank = rank(rank_cols_kernel, met.shape[0], [met, *far], groups, 2 * 10**9)
    terms = local_terms(rows_rank, cols_rank, near, far)
    total = terms[:images]
    for apart in range(subs - 1, 0, -1):
        total = total + across(terms[apart * images : (apart + 1) * images], apart)
    return total


def solution(mesh):
    return jax.shard_map(
        shards,
        mesh=mesh,
        in_specs=(
            P(("group", "narrow"), None),
            P(("group", "narrow")),
            P(),
            P(("group", "narrow"), None),
            P(),
        ),
        out_specs=P(("group", "narrow"), None),
        check_vma=False,
    )
```

```python
import functools
import math

import jax
import jax.numpy as jnp
from jax import lax
from jax.experimental import pallas as pl
from jax.experimental.pallas import tpu as pltpu
from jax.sharding import PartitionSpec as P

P_SIZE = 49
PV = 75
NPROBE = 16
LANES = 128
NORM_AT = PV
ALPHA_AT = PV + 3
FEATURES = 5
STRIDE = PV + FEATURES
TILES = (P_SIZE * STRIDE + 1 + 2 * NPROBE + LANES - 1) // LANES
PACKED = TILES * LANES
TAIL = PACKED - LANES
COUNT_AT = STRIDE
PROBE_AT = COUNT_AT + 1


def layout():
    rest, left = LANES - STRIDE, 2 * (LANES - STRIDE) - STRIDE
    pairs = TILES // 2
    places = [[(tile, 0, 0, STRIDE)] for tile in range(TILES)]
    places += [[(2 * k, STRIDE, 0, rest), (2 * k + 1, STRIDE, rest, STRIDE - rest)] for k in range(pairs)]
    each = STRIDE // left
    for j in range(P_SIZE - len(places)):
        places.append([(2 * (each * j + i) + 1, LANES - left, left * i, left) for i in range(each)])
    return places


OWNER_AT = STRIDE
ROWS = ((1792, 1), (2048, 1), (1024, None))
COLS = ((896, 2), (1024, None))
PREPARED = ((2048, None),)
FILL = 256
SCALE = 2.0 * math.log2(math.e) / (2.0 * PV)
NT = (((1,), (1,)), ((), ()))
NN = (((1,), (0,)), ((), ()))
VMEM = pl.BlockSpec(memory_space=pltpu.VMEM)
SMEM = pl.BlockSpec(memory_space=pltpu.SMEM)


def dot(a, b, dims=NN):
    return lax.dot_general(a, b, dims, preferred_element_type=jnp.float32)


def iota(shape, dim):
    return lax.broadcasted_iota(jnp.int32, shape, dim)


def parts(value):
    hi = value.astype(jnp.bfloat16).astype(jnp.float32)
    rest = value - hi
    mid = rest.astype(jnp.bfloat16).astype(jnp.float32)
    return hi, mid, (rest - mid).astype(jnp.bfloat16).astype(jnp.float32)


def pack_kernel(mine_ref, *refs):
    patches_ref, counts_ref, weights_ref, probes_ref, plan_ref, out_ref, met_ref = refs
    images, wide = patches_ref.shape
    cols, far = met_ref.shape
    plan = plan_ref[...]
    mine = mine_ref[0]
    partner = jnp.sum(jnp.where(iota(plan.shape, 1) == mine, plan, 0), axis=1, keepdims=True)
    line = iota((cols, far), 0)
    source = jnp.zeros((cols, far), jnp.int32)
    for meeting in range(plan.shape[0]):
        here = (line >= meeting * images) & (line < (meeting + 1) * images)
        apart = partner[meeting : meeting + 1, :] ^ mine
        slot = (apart & 1) * (far // images // 2) + (apart >> 1)
        source = jnp.where(here, slot * images + line - meeting * images, source)
    met_ref[...] = (iota((cols, far), 1) == source).astype(jnp.bfloat16)

    shape = (images, LANES)
    lane = iota(shape, 1)
    square = (images, images)
    along = jnp.broadcast_to(counts_ref[...].astype(jnp.float32), square)
    count = jnp.sum(jnp.where(iota(square, 0) == iota(square, 1), along, 0.0), axis=1, keepdims=True)
    weight = jnp.concatenate([weights_ref[...], jnp.zeros((1, LANES - P_SIZE), jnp.float32)], axis=1)
    alpha = weight * (lane.astype(jnp.float32) < count).astype(jnp.float32) / count
    patches = []
    for p in range(P_SIZE):
        values = patches_ref[:, p * PV : min(p * PV + LANES, wide)]
        if values.shape[1] < LANES:
            values = jnp.concatenate([values, jnp.zeros((images, LANES - values.shape[1]), jnp.bfloat16)], axis=1)
        patches.append(jnp.where(lane < PV, values, jnp.bfloat16(0)))
    stacked = jnp.concatenate(patches, axis=0).astype(jnp.float32)
    squares = stacked * stacked
    ones = jnp.ones((LANES, LANES), jnp.bfloat16)
    high = squares.astype(jnp.bfloat16)
    norm = dot(high, ones) + dot((squares - high.astype(jnp.float32)).astype(jnp.bfloat16), ones)
    norms = [part.astype(jnp.bfloat16) for part in parts(-0.5 * norm)]
    alphas = [part.astype(jnp.bfloat16) for part in parts(alpha)[:2]]
    tiles = [None] * (PACKED // LANES)

    def put(values, places):
        for tile, there, here, lanes in places:
            shift = (there - here) % LANES
            moved = pltpu.roll(values, shift, 1) if shift else values
            if lanes < LANES:
                moved = jnp.where((lane >= there) & (lane < there + lanes), moved, jnp.bfloat16(0))
            tiles[tile] = moved if tiles[tile] is None else tiles[tile] + moved

    places = layout()
    for p in range(P_SIZE):
        values = patches[p]
        for step, part in enumerate(norms):
            values = jnp.where(lane == NORM_AT + step, part[p * images : (p + 1) * images], values)
        for step, part in enumerate(alphas):
            values = jnp.where(lane == ALPHA_AT + step, pltpu.roll(part, (ALPHA_AT + step - p) % LANES, 1), values)
        put(values, places[p])
    probe_hi, probe_low, unused = parts(probes_ref[...])
    rest = jnp.concatenate(
        [count, probe_hi, probe_low, jnp.zeros((images, LANES - 1 - 2 * NPROBE), jnp.float32)], axis=1
    )
    put(rest.astype(jnp.bfloat16), [(TILES - 1, COUNT_AT, 0, LANES - STRIDE)])
    for tile, values in enumerate(tiles):
        out_ref[:, tile * LANES : (tile + 1) * LANES] = values


def pack(patches, counts, weights, probes, plan, mine):
    images = patches.shape[0]
    given = (patches, counts[None, :], weights[None, :], probes, plan)
    return pl.pallas_call(
        pack_kernel,
        out_shape=(
            jax.ShapeDtypeStruct((images, PACKED), jnp.bfloat16),
            jax.ShapeDtypeStruct((images * plan.shape[0], images * plan.shape[1]), jnp.bfloat16),
        ),
        in_specs=[SMEM] + [VMEM] * len(given),
        out_specs=(VMEM, VMEM),
        compiler_params=pltpu.CompilerParams(vmem_limit_bytes=8 * 2**20),
        name="pack",
    )(mine, *given)


def order(tail):
    number = tail.shape[0]
    count = tail[:, COUNT_AT : COUNT_AT + 1]
    key = count * number + (number - 1 - iota((number, 1), 0)).astype(jnp.float32)
    square = (number, number)
    key_here = jnp.broadcast_to(key, square)
    key_along = jnp.sum(jnp.where(iota(square, 0) == iota(square, 1), key_here, 0.0), axis=0, keepdims=True)
    rank = jnp.sum((key_here > key_along).astype(jnp.float32), axis=0, keepdims=True)
    chosen = (iota(square, 0).astype(jnp.float32) == rank).astype(jnp.bfloat16)
    patch = iota((number, LANES), 1).astype(jnp.float32)
    valid = jnp.sum((count > patch).astype(jnp.float32), axis=0, keepdims=True)
    before = (iota((LANES, LANES), 0) < iota((LANES, LANES), 1)).astype(jnp.bfloat16)
    first = dot(jnp.broadcast_to(valid, (8, LANES)).astype(jnp.bfloat16), before)
    return chosen, first.astype(jnp.int32)


def owners(chosen):
    number = chosen.shape[0]
    owner = jnp.sum(jnp.where(chosen > 0, iota((number, number), 1).astype(jnp.float32), 0.0), axis=1, keepdims=True)
    return jnp.where(iota((number, LANES), 1) == OWNER_AT, owner, 0.0)


def spread(sorted_ref, owner, first_ref, x_ref, options):
    number = sorted_ref.shape[0]
    lane = iota((number, LANES), 1)
    for p, places in enumerate(layout()):
        values = None
        for tile, there, here, lanes in places:
            moved = sorted_ref[:, tile * LANES : (tile + 1) * LANES]
            if there != here:
                moved = pltpu.roll(moved, (here - there) % LANES, 1)
            values = moved if values is None else jnp.where(lane < here, values, moved)
        values = jnp.where(lane < STRIDE, values.astype(jnp.float32), owner)
        x_ref[pl.ds(first_ref[0, p], number), :] = values
    total = first_ref[0, P_SIZE]
    counts = choose(total, options)
    end = sum(count * size for count, (size, unused) in zip(counts, options))

    def clear(step, unused):
        x_ref[pl.ds(total + step * FILL, FILL), :] = jnp.zeros((FILL, LANES), jnp.float32)
        return unused

    lax.fori_loop(0, (end - total + FILL - 1) // FILL, clear, 0)
    return total, counts


def choose(total, options):
    counts, left = [], 1
    for size, most in options:
        need = (total + size - 1) // size
        fits = left if most is None else jnp.where(need <= most, left, 0)
        counts.append(fits * need)
        left = left - fits
    return counts


def cover(counts, options, step, carry):
    for count, (size, unused) in zip(counts, options):
        carry = lax.fori_loop(0, count, lambda k, c, size=size: step(pl.multiple_of(k * size, LANES), size, c), carry)
    return carry


def rank_rows_kernel(*refs):
    chosen_ref, first_ref = refs[-2:]
    tail = jnp.concatenate([part[:, TAIL : TAIL + LANES] for part in refs[:-2]], axis=0)
    chosen_ref[...], first_ref[...] = order(tail.astype(jnp.float32))


def rank_cols_kernel(met_ref, *refs):
    chosen_ref, first_ref, which_ref, tail_ref = refs[-4:]
    met = met_ref[...]
    tail = dot(met, jnp.concatenate([part[:, TAIL : TAIL + LANES] for part in refs[:-4]], axis=0))
    tail_ref[...] = tail.astype(jnp.bfloat16)
    chosen_ref[...], first_ref[...] = order(tail)
    which_ref[...] = dot(chosen_ref[...], met).astype(jnp.bfloat16)


def rank(kernel, given, number, more, flops):
    shapes = (
        jax.ShapeDtypeStruct((number, number), jnp.bfloat16),
        jax.ShapeDtypeStruct((8, LANES), jnp.int32),
    ) + tuple(jax.ShapeDtypeStruct(shape, jnp.bfloat16) for shape in more)
    return pl.pallas_call(
        kernel,
        out_shape=shapes,
        in_specs=[VMEM] * len(given),
        out_specs=(VMEM,) * len(shapes),
        compiler_params=pltpu.CompilerParams(vmem_limit_bytes=8 * 2**20),
        cost_estimate=pl.CostEstimate(flops=flops, bytes_accessed=10**6, transcendentals=0),
        name="rank",
    )(*given)


def energies(counted, *refs):
    near_number, far_number = counted
    row_given, col_given, row_order, col_order, col_which, tail_ref = refs[:6]
    near_parts = refs[6 : 6 + near_number]
    far_parts = refs[6 + near_number : 6 + near_number + far_number]
    (out_ref, row_sorted, col_sorted, row_x, col_f, col_x, col_u, product, row_first, col_first, sem) = refs[
        6 + near_number + far_number :
    ]
    cols = col_order.shape[0]
    copies = [pltpu.make_async_copy(s, t, sem.at[k]) for k, (s, t) in enumerate(((col_given, col_first), (row_given, row_first)))]
    for copy in copies:
        copy.start()
    product[...] = jnp.zeros_like(product)
    col_sorted[...] = dot(col_which[...], jnp.concatenate([part[...] for part in far_parts], axis=0)).astype(jnp.bfloat16)
    row_sorted[...] = dot(row_order[...], jnp.concatenate([part[...] for part in near_parts], axis=0)).astype(jnp.bfloat16)
    both = (2 * NPROBE, LANES)
    pick_probe = (iota(both, 1) == iota(both, 0) + PROBE_AT).astype(jnp.bfloat16)
    probes = dot(pick_probe, tail_ref[...], NT).astype(jnp.bfloat16)
    col_owner, row_owner = owners(col_order[...]), owners(row_order[...])
    copies[0].wait()
    col_total, col_counts = spread(col_sorted, col_owner, col_first, col_f, COLS)
    copies[1].wait()
    row_total, row_counts = spread(row_sorted, row_owner, row_first, row_x, ROWS)

    line, lane = iota((NPROBE, LANES), 0), iota((NPROBE, LANES), 1)
    pick = (
        ((line == 0) & (lane >= NORM_AT) & (lane < ALPHA_AT))
        | ((line == 1) & (lane >= ALPHA_AT) & (lane < STRIDE))
        | ((line == 2) & (lane == OWNER_AT))
    ).astype(jnp.bfloat16)
    def owned(picked, number, size):
        return (iota((number, size), 0).astype(jnp.float32) == picked[2:3]).astype(jnp.bfloat16)

    def prepare(start, size, unused):
        here = pl.ds(start, size)
        x_cols = col_f[here, :].astype(jnp.bfloat16)
        col_x[here, :] = x_cols
        picked = dot(pick, x_cols, NT)
        mine = dot(probes, owned(picked, cols, size))
        col_u[:, here] = (picked[1:2] * (mine[:NPROBE] + mine[NPROBE:])).astype(jnp.bfloat16)
        return unused

    cover(choose(col_total, PREPARED), PREPARED, prepare, 0)

    def one_row(start, size, unused):
        x_rows = row_x[pl.ds(start, size), :].astype(jnp.bfloat16)
        picked = dot(pick, x_rows, NT)
        row_lane = iota((size, LANES), 1)
        x_rows = jnp.where(
            row_lane < NORM_AT, x_rows, jnp.where(row_lane < ALPHA_AT, jnp.bfloat16(1), jnp.bfloat16(0))
        )

        def one_col(start, size, total):
            here = pl.ds(start, size)
            inner = dot(col_x[here, :], x_rows, NT)
            energy = jnp.exp2((inner + picked[0:1]) * SCALE).astype(jnp.bfloat16)
            return total + dot(col_u[:, here], energy)

        total = cover(col_counts, COLS, one_col, jnp.zeros((NPROBE, size), jnp.float32))
        weighted = jnp.concatenate(parts(total * picked[1:2]), axis=0).astype(jnp.bfloat16)
        sums = dot(weighted, owned(picked, product.shape[1], size), NT)
        product[...] += sums[0:NPROBE] + sums[NPROBE : 2 * NPROBE] + sums[2 * NPROBE :]
        return unused

    cover(row_counts, ROWS, one_row, 0)
    out_ref[...] = product[...].T


def local_terms(rows_rank, cols_rank, near, far):
    row_order, row_first = rows_rank
    col_order, col_first, col_which, col_tail = cols_rank
    rows, cols = row_order.shape[0], col_order.shape[0]
    row_room = rows * P_SIZE + ROWS[1][0] + FILL
    col_room = (cols * P_SIZE // PREPARED[0][0] + 1) * PREPARED[0][0] + FILL
    return pl.pallas_call(
        functools.partial(energies, (len(near), len(far))),
        out_shape=jax.ShapeDtypeStruct((rows, NPROBE), jnp.float32),
        in_specs=[VMEM] * (6 + len(near) + len(far)),
        out_specs=VMEM,
        scratch_shapes=[
            pltpu.VMEM((rows, PACKED), jnp.bfloat16),
            pltpu.VMEM((cols, PACKED), jnp.bfloat16),
            pltpu.VMEM((row_room, LANES), jnp.float32),
            pltpu.VMEM((col_room, LANES), jnp.float32),
            pltpu.VMEM((col_room, LANES), jnp.bfloat16),
            pltpu.VMEM((NPROBE, col_room), jnp.bfloat16),
            pltpu.VMEM((NPROBE, rows), jnp.float32),
            pltpu.SMEM((8, LANES), jnp.int32),
            pltpu.SMEM((8, LANES), jnp.int32),
            pltpu.SemaphoreType.DMA((2,)),
        ],
        compiler_params=pltpu.CompilerParams(vmem_limit_bytes=40 * 2**20),
        name="energies",
    )(row_first, col_first, row_order, col_order, col_which, col_tail, *near, *far)


def shards(patches, counts, weights, probes, plan):
    images = patches.shape[0]
    mine = lax.axis_index("group").reshape(1)
    packed, met = pack(patches, counts, weights, probes, plan, mine)
    groups, subs = lax.axis_size("group"), lax.axis_size("narrow")

    def swap(array, apart):
        return lax.ppermute(array, "group", [(i, i ^ apart) for i in range(groups)])

    def across(array, apart):
        return lax.ppermute(array, "narrow", [(i, i ^ apart) for i in range(subs)])

    even = [packed] + [swap(packed, apart) for apart in range(groups - 2, 0, -2)][::-1]
    far = even + [swap(array, 1) for array in even]
    near = [packed]
    for apart in range(1, subs):
        low = apart & -apart
        near.append(across(near[apart - low], low))
    rows_rank = rank(rank_rows_kernel, near, subs * images, (), 20 * 10**9)
    cols = met.shape[0]
    cols_rank = rank(rank_cols_kernel, [met, *far], cols, (met.shape, (cols, LANES)), 2 * 10**9)
    terms = local_terms(rows_rank, cols_rank, near, far)
    total = terms[:images]
    for apart in range(subs - 1, 0, -1):
        total = total + across(terms[apart * images : (apart + 1) * images], apart)
    return total


def solution(mesh):
    return jax.shard_map(
        shards,
        mesh=mesh,
        in_specs=(
            P(("group", "narrow"), None),
            P(("group", "narrow")),
            P(),
            P(("group", "narrow"), None),
            P(),
        ),
        out_specs=P(("group", "narrow"), None),
        check_vma=False,
    )
```

```python
import functools
import math

import jax
import jax.numpy as jnp
from jax import lax
from jax.experimental import pallas as pl
from jax.experimental.pallas import tpu as pltpu
from jax.sharding import PartitionSpec as P

P_SIZE = 49
PV = 75
NPROBE = 16
LANES = 128
NORM_AT = PV
ALPHA_AT = PV + 3
FEATURES = 5
STRIDE = PV + FEATURES
TILES = (P_SIZE * STRIDE + 1 + 2 * NPROBE + LANES - 1) // LANES
PACKED = TILES * LANES
TAIL = PACKED - LANES
COUNT_AT = STRIDE
PROBE_AT = COUNT_AT + 1


def layout():
    rest, left = LANES - STRIDE, 2 * (LANES - STRIDE) - STRIDE
    pairs = TILES // 2
    places = [[(tile, 0, 0, STRIDE)] for tile in range(TILES)]
    places += [[(2 * k, STRIDE, 0, rest), (2 * k + 1, STRIDE, rest, STRIDE - rest)] for k in range(pairs)]
    each = STRIDE // left
    for j in range(P_SIZE - len(places)):
        places.append([(2 * (each * j + i) + 1, LANES - left, left * i, left) for i in range(each)])
    return places


OWNER_AT = STRIDE
ROWS = ((1664, 1), (1792, 1), (2048, 1), (1024, None))
COLS = ((896, 2), (1024, None))
PREPARED = ((2048, None),)
FILL = 256
SCALE = 2.0 * math.log2(math.e) / (2.0 * PV)
NT = (((1,), (1,)), ((), ()))
NN = (((1,), (0,)), ((), ()))
VMEM = pl.BlockSpec(memory_space=pltpu.VMEM)
SMEM = pl.BlockSpec(memory_space=pltpu.SMEM)


def dot(a, b, dims=NN):
    return lax.dot_general(a, b, dims, preferred_element_type=jnp.float32)


def iota(shape, dim):
    return lax.broadcasted_iota(jnp.int32, shape, dim)


def parts(value):
    hi = value.astype(jnp.bfloat16).astype(jnp.float32)
    rest = value - hi
    mid = rest.astype(jnp.bfloat16).astype(jnp.float32)
    return hi, mid, (rest - mid).astype(jnp.bfloat16).astype(jnp.float32)


def pack_kernel(mine_ref, *refs):
    patches_ref, counts_ref, weights_ref, probes_ref, plan_ref, out_ref, met_ref = refs
    images, wide = patches_ref.shape
    cols, far = met_ref.shape
    plan = plan_ref[...]
    mine = mine_ref[0]
    partner = jnp.sum(jnp.where(iota(plan.shape, 1) == mine, plan, 0), axis=1, keepdims=True)
    line = iota((cols, far), 0)
    source = jnp.zeros((cols, far), jnp.int32)
    for meeting in range(plan.shape[0]):
        here = (line >= meeting * images) & (line < (meeting + 1) * images)
        apart = partner[meeting : meeting + 1, :] ^ mine
        slot = (apart & 1) * (far // images // 2) + (apart >> 1)
        source = jnp.where(here, slot * images + line - meeting * images, source)
    met_ref[...] = (iota((cols, far), 1) == source).astype(jnp.bfloat16)

    shape = (images, LANES)
    lane = iota(shape, 1)
    square = (images, images)
    along = jnp.broadcast_to(counts_ref[...].astype(jnp.float32), square)
    count = jnp.sum(jnp.where(iota(square, 0) == iota(square, 1), along, 0.0), axis=1, keepdims=True)
    weight = jnp.concatenate([weights_ref[...], jnp.zeros((1, LANES - P_SIZE), jnp.float32)], axis=1)
    alpha = weight * (lane.astype(jnp.float32) < count).astype(jnp.float32) / count
    patches = []
    for p in range(P_SIZE):
        values = patches_ref[:, p * PV : min(p * PV + LANES, wide)]
        if values.shape[1] < LANES:
            values = jnp.concatenate([values, jnp.zeros((images, LANES - values.shape[1]), jnp.bfloat16)], axis=1)
        patches.append(jnp.where(lane < PV, values, jnp.bfloat16(0)))
    stacked = jnp.concatenate(patches, axis=0).astype(jnp.float32)
    squares = stacked * stacked
    ones = jnp.ones((LANES, LANES), jnp.bfloat16)
    high = squares.astype(jnp.bfloat16)
    norm = dot(high, ones) + dot((squares - high.astype(jnp.float32)).astype(jnp.bfloat16), ones)
    norms = [part.astype(jnp.bfloat16) for part in parts(-0.5 * norm)]
    alphas = [part.astype(jnp.bfloat16) for part in parts(alpha)[:2]]
    tiles = [None] * (PACKED // LANES)

    def put(values, places):
        for tile, there, here, lanes in places:
            shift = (there - here) % LANES
            moved = pltpu.roll(values, shift, 1) if shift else values
            if lanes < LANES:
                moved = jnp.where((lane >= there) & (lane < there + lanes), moved, jnp.bfloat16(0))
            tiles[tile] = moved if tiles[tile] is None else tiles[tile] + moved

    places = layout()
    for p in range(P_SIZE):
        values = patches[p]
        for step, part in enumerate(norms):
            values = jnp.where(lane == NORM_AT + step, part[p * images : (p + 1) * images], values)
        for step, part in enumerate(alphas):
            values = jnp.where(lane == ALPHA_AT + step, pltpu.roll(part, (ALPHA_AT + step - p) % LANES, 1), values)
        put(values, places[p])
    probe_hi, probe_low, unused = parts(probes_ref[...])
    rest = jnp.concatenate(
        [count, probe_hi, probe_low, jnp.zeros((images, LANES - 1 - 2 * NPROBE), jnp.float32)], axis=1
    )
    put(rest.astype(jnp.bfloat16), [(TILES - 1, COUNT_AT, 0, LANES - STRIDE)])
    for tile, values in enumerate(tiles):
        out_ref[:, tile * LANES : (tile + 1) * LANES] = values


def pack(patches, counts, weights, probes, plan, mine):
    images = patches.shape[0]
    given = (patches, counts[None, :], weights[None, :], probes, plan)
    return pl.pallas_call(
        pack_kernel,
        out_shape=(
            jax.ShapeDtypeStruct((images, PACKED), jnp.bfloat16),
            jax.ShapeDtypeStruct((images * plan.shape[0], images * plan.shape[1]), jnp.bfloat16),
        ),
        in_specs=[SMEM] + [VMEM] * len(given),
        out_specs=(VMEM, VMEM),
        compiler_params=pltpu.CompilerParams(vmem_limit_bytes=8 * 2**20),
        name="pack",
    )(mine, *given)


def order(tail):
    number = tail.shape[0]
    count = tail[:, COUNT_AT : COUNT_AT + 1]
    key = count * number + (number - 1 - iota((number, 1), 0)).astype(jnp.float32)
    square = (number, number)
    key_here = jnp.broadcast_to(key, square)
    key_along = jnp.sum(jnp.where(iota(square, 0) == iota(square, 1), key_here, 0.0), axis=0, keepdims=True)
    rank = jnp.sum((key_here > key_along).astype(jnp.float32), axis=0, keepdims=True)
    chosen = (iota(square, 0).astype(jnp.float32) == rank).astype(jnp.bfloat16)
    patch = iota((number, LANES), 1).astype(jnp.float32)
    valid = jnp.sum((count > patch).astype(jnp.float32), axis=0, keepdims=True)
    before = (iota((LANES, LANES), 0) < iota((LANES, LANES), 1)).astype(jnp.bfloat16)
    first = dot(jnp.broadcast_to(valid, (8, LANES)).astype(jnp.bfloat16), before)
    return chosen, first.astype(jnp.int32)


def owners(chosen):
    number = chosen.shape[0]
    owner = jnp.sum(jnp.where(chosen > 0, iota((number, number), 1).astype(jnp.float32), 0.0), axis=1, keepdims=True)
    return jnp.where(iota((number, LANES), 1) == OWNER_AT, owner, 0.0)


def spread(sorted_ref, owner, first_ref, x_ref, options):
    number = sorted_ref.shape[0]
    lane = iota((number, LANES), 1)
    for p, places in enumerate(layout()):
        values = None
        for tile, there, here, lanes in places:
            moved = sorted_ref[:, tile * LANES : (tile + 1) * LANES]
            if there != here:
                moved = pltpu.roll(moved, (here - there) % LANES, 1)
            values = moved if values is None else jnp.where(lane < here, values, moved)
        values = jnp.where(lane < STRIDE, values.astype(jnp.float32), owner)
        x_ref[pl.ds(first_ref[0, p], number), :] = values
    total = first_ref[0, P_SIZE]
    counts = choose(total, options)
    end = sum(count * size for count, (size, unused) in zip(counts, options))

    def clear(step, unused):
        x_ref[pl.ds(total + step * FILL, FILL), :] = jnp.zeros((FILL, LANES), jnp.float32)
        return unused

    lax.fori_loop(0, (end - total + FILL - 1) // FILL, clear, 0)
    return total, counts


def choose(total, options):
    counts, left = [], 1
    for size, most in options:
        need = (total + size - 1) // size
        fits = left if most is None else jnp.where(need <= most, left, 0)
        counts.append(fits * need)
        left = left - fits
    return counts


def cover(counts, options, step, carry):
    for count, (size, unused) in zip(counts, options):
        carry = lax.fori_loop(0, count, lambda k, c, size=size: step(pl.multiple_of(k * size, LANES), size, c), carry)
    return carry


def rank_rows_kernel(*refs):
    chosen_ref, first_ref = refs[-2:]
    tail = jnp.concatenate([part[:, TAIL : TAIL + LANES] for part in refs[:-2]], axis=0)
    chosen_ref[...], first_ref[...] = order(tail.astype(jnp.float32))


def rank_cols_kernel(met_ref, *refs):
    chosen_ref, first_ref, which_ref, tail_ref = refs[-4:]
    met = met_ref[...]
    tail = dot(met, jnp.concatenate([part[:, TAIL : TAIL + LANES] for part in refs[:-4]], axis=0))
    tail_ref[...] = tail.astype(jnp.bfloat16)
    chosen_ref[...], first_ref[...] = order(tail)
    which_ref[...] = dot(chosen_ref[...], met).astype(jnp.bfloat16)


def rank(kernel, given, number, more, flops):
    shapes = (
        jax.ShapeDtypeStruct((number, number), jnp.bfloat16),
        jax.ShapeDtypeStruct((8, LANES), jnp.int32),
    ) + tuple(jax.ShapeDtypeStruct(shape, jnp.bfloat16) for shape in more)
    return pl.pallas_call(
        kernel,
        out_shape=shapes,
        in_specs=[VMEM] * len(given),
        out_specs=(VMEM,) * len(shapes),
        compiler_params=pltpu.CompilerParams(vmem_limit_bytes=8 * 2**20),
        cost_estimate=pl.CostEstimate(flops=flops, bytes_accessed=10**6, transcendentals=0),
        name="rank",
    )(*given)


def energies(counted, *refs):
    near_number, far_number = counted
    row_given, col_given, row_order, col_order, col_which, tail_ref = refs[:6]
    near_parts = refs[6 : 6 + near_number]
    far_parts = refs[6 + near_number : 6 + near_number + far_number]
    (out_ref, row_sorted, col_sorted, row_x, col_f, col_x, col_u, product, row_first, col_first, sem) = refs[
        6 + near_number + far_number :
    ]
    cols = col_order.shape[0]
    copies = [pltpu.make_async_copy(s, t, sem.at[k]) for k, (s, t) in enumerate(((col_given, col_first), (row_given, row_first)))]
    for copy in copies:
        copy.start()
    product[...] = jnp.zeros_like(product)
    col_sorted[...] = dot(col_which[...], jnp.concatenate([part[...] for part in far_parts], axis=0)).astype(jnp.bfloat16)
    row_sorted[...] = dot(row_order[...], jnp.concatenate([part[...] for part in near_parts], axis=0)).astype(jnp.bfloat16)
    both = (2 * NPROBE, LANES)
    pick_probe = (iota(both, 1) == iota(both, 0) + PROBE_AT).astype(jnp.bfloat16)
    probes = dot(pick_probe, tail_ref[...], NT).astype(jnp.bfloat16)
    col_owner, row_owner = owners(col_order[...]), owners(row_order[...])
    copies[0].wait()
    col_total, col_counts = spread(col_sorted, col_owner, col_first, col_f, COLS)
    copies[1].wait()
    row_total, row_counts = spread(row_sorted, row_owner, row_first, row_x, ROWS)

    line, lane = iota((NPROBE, LANES), 0), iota((NPROBE, LANES), 1)
    pick = (
        ((line == 0) & (lane >= NORM_AT) & (lane < ALPHA_AT))
        | ((line == 1) & (lane >= ALPHA_AT) & (lane < STRIDE))
        | ((line == 2) & (lane == OWNER_AT))
    ).astype(jnp.bfloat16)
    def owned(picked, number, size):
        return (iota((number, size), 0).astype(jnp.float32) == picked[2:3]).astype(jnp.bfloat16)

    def prepare(start, size, unused):
        here = pl.ds(start, size)
        x_cols = col_f[here, :].astype(jnp.bfloat16)
        col_x[here, :] = x_cols
        picked = dot(pick, x_cols, NT)
        mine = dot(probes, owned(picked, cols, size))
        col_u[:, here] = (picked[1:2] * (mine[:NPROBE] + mine[NPROBE:])).astype(jnp.bfloat16)
        return unused

    cover(choose(col_total, PREPARED), PREPARED, prepare, 0)

    def one_row(start, size, unused):
        x_rows = row_x[pl.ds(start, size), :].astype(jnp.bfloat16)
        picked = dot(pick, x_rows, NT)
        row_lane = iota((size, LANES), 1)
        x_rows = jnp.where(
            row_lane < NORM_AT, x_rows, jnp.where(row_lane < ALPHA_AT, jnp.bfloat16(1), jnp.bfloat16(0))
        )

        def one_col(start, size, total):
            here = pl.ds(start, size)
            inner = dot(col_x[here, :], x_rows, NT)
            energy = jnp.exp2((inner + picked[0:1]) * SCALE).astype(jnp.bfloat16)
            return total + dot(col_u[:, here], energy)

        total = cover(col_counts, COLS, one_col, jnp.zeros((NPROBE, size), jnp.float32))
        weighted = jnp.concatenate(parts(total * picked[1:2]), axis=0).astype(jnp.bfloat16)
        sums = dot(weighted, owned(picked, product.shape[1], size), NT)
        product[...] += sums[0:NPROBE] + sums[NPROBE : 2 * NPROBE] + sums[2 * NPROBE :]
        return unused

    cover(row_counts, ROWS, one_row, 0)
    out_ref[...] = product[...].T


def local_terms(rows_rank, cols_rank, near, far):
    row_order, row_first = rows_rank
    col_order, col_first, col_which, col_tail = cols_rank
    rows, cols = row_order.shape[0], col_order.shape[0]
    row_room = rows * P_SIZE + ROWS[2][0] + FILL
    col_room = (cols * P_SIZE // PREPARED[0][0] + 1) * PREPARED[0][0] + FILL
    return pl.pallas_call(
        functools.partial(energies, (len(near), len(far))),
        out_shape=jax.ShapeDtypeStruct((rows, NPROBE), jnp.float32),
        in_specs=[VMEM] * (6 + len(near) + len(far)),
        out_specs=VMEM,
        scratch_shapes=[
            pltpu.VMEM((rows, PACKED), jnp.bfloat16),
            pltpu.VMEM((cols, PACKED), jnp.bfloat16),
            pltpu.VMEM((row_room, LANES), jnp.float32),
            pltpu.VMEM((col_room, LANES), jnp.float32),
            pltpu.VMEM((col_room, LANES), jnp.bfloat16),
            pltpu.VMEM((NPROBE, col_room), jnp.bfloat16),
            pltpu.VMEM((NPROBE, rows), jnp.float32),
            pltpu.SMEM((8, LANES), jnp.int32),
            pltpu.SMEM((8, LANES), jnp.int32),
            pltpu.SemaphoreType.DMA((2,)),
        ],
        compiler_params=pltpu.CompilerParams(vmem_limit_bytes=40 * 2**20),
        name="energies",
    )(row_first, col_first, row_order, col_order, col_which, col_tail, *near, *far)


def shards(patches, counts, weights, probes, plan):
    images = patches.shape[0]
    mine = lax.axis_index("group").reshape(1)
    packed, met = pack(patches, counts, weights, probes, plan, mine)
    groups, subs = lax.axis_size("group"), lax.axis_size("narrow")

    def swap(array, apart):
        return lax.ppermute(array, "group", [(i, i ^ apart) for i in range(groups)])

    def across(array, apart):
        return lax.ppermute(array, "narrow", [(i, i ^ apart) for i in range(subs)])

    even = [packed] + [swap(packed, apart) for apart in range(groups - 2, 0, -2)][::-1]
    far = even + [swap(array, 1) for array in even]
    near = [packed]
    for apart in range(1, subs):
        low = apart & -apart
        near.append(across(near[apart - low], low))
    rows_rank = rank(rank_rows_kernel, near, subs * images, (), 20 * 10**9)
    cols = met.shape[0]
    cols_rank = rank(rank_cols_kernel, [met, *far], cols, (met.shape, (cols, LANES)), 2 * 10**9)
    terms = local_terms(rows_rank, cols_rank, near, far)
    total = terms[:images]
    for apart in range(subs - 1, 0, -1):
        total = total + across(terms[apart * images : (apart + 1) * images], apart)
    return total


def solution(mesh):
    return jax.shard_map(
        shards,
        mesh=mesh,
        in_specs=(
            P(("group", "narrow"), None),
            P(("group", "narrow")),
            P(),
            P(("group", "narrow"), None),
            P(),
        ),
        out_specs=P(("group", "narrow"), None),
        check_vma=False,
    )
```

```python
import functools
import math

import jax
import jax.numpy as jnp
from jax import lax
from jax.experimental import pallas as pl
from jax.experimental.pallas import tpu as pltpu
from jax.sharding import PartitionSpec as P

P_SIZE = 49
PV = 75
NPROBE = 16
LANES = 128
NORM_AT = PV
ALPHA_AT = PV + 3
FEATURES = 5
STRIDE = PV + FEATURES
TILES = (P_SIZE * STRIDE + 1 + 2 * NPROBE + LANES - 1) // LANES
PACKED = TILES * LANES
TAIL = PACKED - LANES
COUNT_AT = STRIDE
PROBE_AT = COUNT_AT + 1


def layout():
    rest, left = LANES - STRIDE, 2 * (LANES - STRIDE) - STRIDE
    pairs = TILES // 2
    places = [[(tile, 0, 0, STRIDE)] for tile in range(TILES)]
    places += [[(2 * k, STRIDE, 0, rest), (2 * k + 1, STRIDE, rest, STRIDE - rest)] for k in range(pairs)]
    each = STRIDE // left
    for j in range(P_SIZE - len(places)):
        places.append([(2 * (each * j + i) + 1, LANES - left, left * i, left) for i in range(each)])
    return places


OWNER_AT = STRIDE
ROWS = ((1792, 1), (2048, 1), (1024, None))
COLS = ((896, 2), (1024, None))
PREPARED = ((2048, None),)
FILL = 256
SCALE = 2.0 * math.log2(math.e) / (2.0 * PV)
NT = (((1,), (1,)), ((), ()))
NN = (((1,), (0,)), ((), ()))
VMEM = pl.BlockSpec(memory_space=pltpu.VMEM)
SMEM = pl.BlockSpec(memory_space=pltpu.SMEM)


def dot(a, b, dims=NN):
    return lax.dot_general(a, b, dims, preferred_element_type=jnp.float32)


def iota(shape, dim):
    return lax.broadcasted_iota(jnp.int32, shape, dim)


def parts(value):
    hi = value.astype(jnp.bfloat16).astype(jnp.float32)
    rest = value - hi
    mid = rest.astype(jnp.bfloat16).astype(jnp.float32)
    return hi, mid, (rest - mid).astype(jnp.bfloat16).astype(jnp.float32)


def pack_kernel(mine_ref, *refs):
    patches_ref, counts_ref, weights_ref, probes_ref, plan_ref, out_ref, met_ref = refs
    images, wide = patches_ref.shape
    cols, far = met_ref.shape
    plan = plan_ref[...]
    mine = mine_ref[0]
    partner = jnp.sum(jnp.where(iota(plan.shape, 1) == mine, plan, 0), axis=1, keepdims=True)
    line = iota((cols, far), 0)
    source = jnp.zeros((cols, far), jnp.int32)
    for meeting in range(plan.shape[0]):
        here = (line >= meeting * images) & (line < (meeting + 1) * images)
        apart = partner[meeting : meeting + 1, :] ^ mine
        slot = (apart & 1) * (far // images // 2) + (apart >> 1)
        source = jnp.where(here, slot * images + line - meeting * images, source)
    met_ref[...] = (iota((cols, far), 1) == source).astype(jnp.bfloat16)

    shape = (images, LANES)
    lane = iota(shape, 1)
    square = (images, images)
    along = jnp.broadcast_to(counts_ref[...].astype(jnp.float32), square)
    count = jnp.sum(jnp.where(iota(square, 0) == iota(square, 1), along, 0.0), axis=1, keepdims=True)
    weight = jnp.concatenate([weights_ref[...], jnp.zeros((1, LANES - P_SIZE), jnp.float32)], axis=1)
    alpha = weight * (lane.astype(jnp.float32) < count).astype(jnp.float32) / count
    patches = []
    for p in range(P_SIZE):
        values = patches_ref[:, p * PV : min(p * PV + LANES, wide)]
        if values.shape[1] < LANES:
            values = jnp.concatenate([values, jnp.zeros((images, LANES - values.shape[1]), jnp.bfloat16)], axis=1)
        patches.append(jnp.where(lane < PV, values, jnp.bfloat16(0)))
    stacked = jnp.concatenate(patches, axis=0).astype(jnp.float32)
    squares = stacked * stacked
    ones = jnp.ones((LANES, LANES), jnp.bfloat16)
    high = squares.astype(jnp.bfloat16)
    norm = dot(high, ones) + dot((squares - high.astype(jnp.float32)).astype(jnp.bfloat16), ones)
    norms = [part.astype(jnp.bfloat16) for part in parts(-0.5 * norm)]
    alphas = [part.astype(jnp.bfloat16) for part in parts(alpha)[:2]]
    tiles = [None] * (PACKED // LANES)

    def put(values, places):
        for tile, there, here, lanes in places:
            shift = (there - here) % LANES
            moved = pltpu.roll(values, shift, 1) if shift else values
            if lanes < LANES:
                moved = jnp.where((lane >= there) & (lane < there + lanes), moved, jnp.bfloat16(0))
            tiles[tile] = moved if tiles[tile] is None else tiles[tile] + moved

    places = layout()
    for p in range(P_SIZE):
        values = patches[p]
        for step, part in enumerate(norms):
            values = jnp.where(lane == NORM_AT + step, part[p * images : (p + 1) * images], values)
        for step, part in enumerate(alphas):
            values = jnp.where(lane == ALPHA_AT + step, pltpu.roll(part, (ALPHA_AT + step - p) % LANES, 1), values)
        put(values, places[p])
    probe_hi, probe_low, unused = parts(probes_ref[...])
    rest = jnp.concatenate(
        [count, probe_hi, probe_low, jnp.zeros((images, LANES - 1 - 2 * NPROBE), jnp.float32)], axis=1
    )
    put(rest.astype(jnp.bfloat16), [(TILES - 1, COUNT_AT, 0, LANES - STRIDE)])
    for tile, values in enumerate(tiles):
        out_ref[:, tile * LANES : (tile + 1) * LANES] = values


def pack(patches, counts, weights, probes, plan, mine):
    images = patches.shape[0]
    given = (patches, counts[None, :], weights[None, :], probes, plan)
    return pl.pallas_call(
        pack_kernel,
        out_shape=(
            jax.ShapeDtypeStruct((images, PACKED), jnp.bfloat16),
            jax.ShapeDtypeStruct((images * plan.shape[0], images * plan.shape[1]), jnp.bfloat16),
        ),
        in_specs=[SMEM] + [VMEM] * len(given),
        out_specs=(VMEM, VMEM),
        compiler_params=pltpu.CompilerParams(vmem_limit_bytes=8 * 2**20),
        name="pack",
    )(mine, *given)


def order(tail):
    number = tail.shape[0]
    count = tail[:, COUNT_AT : COUNT_AT + 1]
    key = count * number + (number - 1 - iota((number, 1), 0)).astype(jnp.float32)
    square = (number, number)
    key_here = jnp.broadcast_to(key, square)
    key_along = jnp.sum(jnp.where(iota(square, 0) == iota(square, 1), key_here, 0.0), axis=0, keepdims=True)
    rank = jnp.sum((key_here > key_along).astype(jnp.float32), axis=0, keepdims=True)
    chosen = (iota(square, 0).astype(jnp.float32) == rank).astype(jnp.bfloat16)
    patch = iota((number, LANES), 1).astype(jnp.float32)
    valid = jnp.sum((count > patch).astype(jnp.float32), axis=0, keepdims=True)
    before = (iota((LANES, LANES), 0) < iota((LANES, LANES), 1)).astype(jnp.bfloat16)
    first = dot(jnp.broadcast_to(valid, (8, LANES)).astype(jnp.bfloat16), before)
    return chosen, first.astype(jnp.int32)


def owners(chosen):
    number = chosen.shape[0]
    owner = jnp.sum(jnp.where(chosen > 0, iota((number, number), 1).astype(jnp.float32), 0.0), axis=1, keepdims=True)
    return jnp.where(iota((number, LANES), 1) == OWNER_AT, owner, 0.0)


def spread(sorted_ref, owner, first_ref, x_ref, options):
    number = sorted_ref.shape[0]
    lane = iota((number, LANES), 1)
    for p, places in enumerate(layout()):
        values = None
        for tile, there, here, lanes in places:
            moved = sorted_ref[:, tile * LANES : (tile + 1) * LANES]
            if there != here:
                moved = pltpu.roll(moved, (here - there) % LANES, 1)
            values = moved if values is None else jnp.where(lane < here, values, moved)
        values = jnp.where(lane < STRIDE, values.astype(jnp.float32), owner)
        x_ref[pl.ds(first_ref[0, p], number), :] = values
    total = first_ref[0, P_SIZE]
    counts = choose(total, options)
    end = sum(count * size for count, (size, unused) in zip(counts, options))

    def clear(step, unused):
        x_ref[pl.ds(total + step * FILL, FILL), :] = jnp.zeros((FILL, LANES), jnp.float32)
        return unused

    lax.fori_loop(0, (end - total + FILL - 1) // FILL, clear, 0)
    return total, counts


def choose(total, options):
    counts, left = [], 1
    for size, most in options:
        need = (total + size - 1) // size
        fits = left if most is None else jnp.where(need <= most, left, 0)
        counts.append(fits * need)
        left = left - fits
    if len(options) == 2 and options[0][1] == 2:
        sizes = options[0][0], options[1][0]
        both = jnp.where((total > 2 * sizes[0]) & (total <= sum(sizes)), 1, 0)
        counts = [jnp.where(both == 1, 1, count) for count in counts]
    return counts


def cover(counts, options, step, carry):
    base = 0
    for count, (size, unused) in zip(counts, options):
        carry = lax.fori_loop(
            0, count, lambda k, c, size=size, base=base: step(pl.multiple_of(base + k * size, LANES), size, c), carry
        )
        base = base + count * size
    return carry


def rank_rows_kernel(*refs):
    chosen_ref, first_ref = refs[-2:]
    tail = jnp.concatenate([part[:, TAIL : TAIL + LANES] for part in refs[:-2]], axis=0)
    chosen_ref[...], first_ref[...] = order(tail.astype(jnp.float32))


def rank_cols_kernel(met_ref, *refs):
    chosen_ref, first_ref, which_ref, tail_ref = refs[-4:]
    met = met_ref[...]
    tail = dot(met, jnp.concatenate([part[:, TAIL : TAIL + LANES] for part in refs[:-4]], axis=0))
    tail_ref[...] = tail.astype(jnp.bfloat16)
    chosen_ref[...], first_ref[...] = order(tail)
    which_ref[...] = dot(chosen_ref[...], met).astype(jnp.bfloat16)


def rank(kernel, given, number, more, flops):
    shapes = (
        jax.ShapeDtypeStruct((number, number), jnp.bfloat16),
        jax.ShapeDtypeStruct((8, LANES), jnp.int32),
    ) + tuple(jax.ShapeDtypeStruct(shape, jnp.bfloat16) for shape in more)
    return pl.pallas_call(
        kernel,
        out_shape=shapes,
        in_specs=[VMEM] * len(given),
        out_specs=(VMEM,) * len(shapes),
        compiler_params=pltpu.CompilerParams(vmem_limit_bytes=8 * 2**20),
        cost_estimate=pl.CostEstimate(flops=flops, bytes_accessed=10**6, transcendentals=0),
        name="rank",
    )(*given)


def energies(counted, *refs):
    near_number, far_number = counted
    row_given, col_given, row_order, col_order, col_which, tail_ref = refs[:6]
    near_parts = refs[6 : 6 + near_number]
    far_parts = refs[6 + near_number : 6 + near_number + far_number]
    (out_ref, row_sorted, col_sorted, row_x, col_f, col_x, col_u, product, row_first, col_first, sem) = refs[
        6 + near_number + far_number :
    ]
    cols = col_order.shape[0]
    copies = [pltpu.make_async_copy(s, t, sem.at[k]) for k, (s, t) in enumerate(((col_given, col_first), (row_given, row_first)))]
    for copy in copies:
        copy.start()
    product[...] = jnp.zeros_like(product)
    col_sorted[...] = dot(col_which[...], jnp.concatenate([part[...] for part in far_parts], axis=0)).astype(jnp.bfloat16)
    row_sorted[...] = dot(row_order[...], jnp.concatenate([part[...] for part in near_parts], axis=0)).astype(jnp.bfloat16)
    both = (2 * NPROBE, LANES)
    pick_probe = (iota(both, 1) == iota(both, 0) + PROBE_AT).astype(jnp.bfloat16)
    probes = dot(pick_probe, tail_ref[...], NT).astype(jnp.bfloat16)
    col_owner, row_owner = owners(col_order[...]), owners(row_order[...])
    copies[0].wait()
    col_total, col_counts = spread(col_sorted, col_owner, col_first, col_f, COLS)
    copies[1].wait()
    row_total, row_counts = spread(row_sorted, row_owner, row_first, row_x, ROWS)

    line, lane = iota((NPROBE, LANES), 0), iota((NPROBE, LANES), 1)
    pick = (
        ((line == 0) & (lane >= NORM_AT) & (lane < ALPHA_AT))
        | ((line == 1) & (lane >= ALPHA_AT) & (lane < STRIDE))
        | ((line == 2) & (lane == OWNER_AT))
    ).astype(jnp.bfloat16)
    def owned(picked, number, size):
        return (iota((number, size), 0).astype(jnp.float32) == picked[2:3]).astype(jnp.bfloat16)

    def prepare(start, size, unused):
        here = pl.ds(start, size)
        x_cols = col_f[here, :].astype(jnp.bfloat16)
        col_x[here, :] = x_cols
        picked = dot(pick, x_cols, NT)
        mine = dot(probes, owned(picked, cols, size))
        col_u[:, here] = (picked[1:2] * (mine[:NPROBE] + mine[NPROBE:])).astype(jnp.bfloat16)
        return unused

    cover(choose(col_total, PREPARED), PREPARED, prepare, 0)

    def one_row(start, size, unused):
        x_rows = row_x[pl.ds(start, size), :].astype(jnp.bfloat16)
        picked = dot(pick, x_rows, NT)
        row_lane = iota((size, LANES), 1)
        x_rows = jnp.where(
            row_lane < NORM_AT, x_rows, jnp.where(row_lane < ALPHA_AT, jnp.bfloat16(1), jnp.bfloat16(0))
        )

        def one_col(start, size, total):
            here = pl.ds(start, size)
            inner = dot(col_x[here, :], x_rows, NT)
            energy = jnp.exp2((inner + picked[0:1]) * SCALE).astype(jnp.bfloat16)
            return total + dot(col_u[:, here], energy)

        total = cover(col_counts, COLS, one_col, jnp.zeros((NPROBE, size), jnp.float32))
        weighted = jnp.concatenate(parts(total * picked[1:2]), axis=0).astype(jnp.bfloat16)
        sums = dot(weighted, owned(picked, product.shape[1], size), NT)
        product[...] += sums[0:NPROBE] + sums[NPROBE : 2 * NPROBE] + sums[2 * NPROBE :]
        return unused

    cover(row_counts, ROWS, one_row, 0)
    out_ref[...] = product[...].T


def local_terms(rows_rank, cols_rank, near, far):
    row_order, row_first = rows_rank
    col_order, col_first, col_which, col_tail = cols_rank
    rows, cols = row_order.shape[0], col_order.shape[0]
    row_room = rows * P_SIZE + ROWS[1][0] + FILL
    col_room = (cols * P_SIZE // PREPARED[0][0] + 1) * PREPARED[0][0] + FILL
    return pl.pallas_call(
        functools.partial(energies, (len(near), len(far))),
        out_shape=jax.ShapeDtypeStruct((rows, NPROBE), jnp.float32),
        in_specs=[VMEM] * (6 + len(near) + len(far)),
        out_specs=VMEM,
        scratch_shapes=[
            pltpu.VMEM((rows, PACKED), jnp.bfloat16),
            pltpu.VMEM((cols, PACKED), jnp.bfloat16),
            pltpu.VMEM((row_room, LANES), jnp.float32),
            pltpu.VMEM((col_room, LANES), jnp.float32),
            pltpu.VMEM((col_room, LANES), jnp.bfloat16),
            pltpu.VMEM((NPROBE, col_room), jnp.bfloat16),
            pltpu.VMEM((NPROBE, rows), jnp.float32),
            pltpu.SMEM((8, LANES), jnp.int32),
            pltpu.SMEM((8, LANES), jnp.int32),
            pltpu.SemaphoreType.DMA((2,)),
        ],
        compiler_params=pltpu.CompilerParams(vmem_limit_bytes=40 * 2**20),
        name="energies",
    )(row_first, col_first, row_order, col_order, col_which, col_tail, *near, *far)


def shards(patches, counts, weights, probes, plan):
    images = patches.shape[0]
    mine = lax.axis_index("group").reshape(1)
    packed, met = pack(patches, counts, weights, probes, plan, mine)
    groups, subs = lax.axis_size("group"), lax.axis_size("narrow")

    def swap(array, apart):
        return lax.ppermute(array, "group", [(i, i ^ apart) for i in range(groups)])

    def across(array, apart):
        return lax.ppermute(array, "narrow", [(i, i ^ apart) for i in range(subs)])

    even = [packed] + [swap(packed, apart) for apart in range(groups - 2, 0, -2)][::-1]
    far = even + [swap(array, 1) for array in even]
    near = [packed]
    for apart in range(1, subs):
        low = apart & -apart
        near.append(across(near[apart - low], low))
    rows_rank = rank(rank_rows_kernel, near, subs * images, (), 20 * 10**9)
    cols = met.shape[0]
    cols_rank = rank(rank_cols_kernel, [met, *far], cols, (met.shape, (cols, LANES)), 2 * 10**9)
    terms = local_terms(rows_rank, cols_rank, near, far)
    total = terms[:images]
    for apart in range(subs - 1, 0, -1):
        total = total + across(terms[apart * images : (apart + 1) * images], apart)
    return total


def solution(mesh):
    return jax.shard_map(
        shards,
        mesh=mesh,
        in_specs=(
            P(("group", "narrow"), None),
            P(("group", "narrow")),
            P(),
            P(("group", "narrow"), None),
            P(),
        ),
        out_specs=P(("group", "narrow"), None),
        check_vma=False,
    )
```

```python
import functools
import math

import jax
import jax.numpy as jnp
from jax import lax
from jax.experimental import pallas as pl
from jax.experimental.pallas import tpu as pltpu
from jax.sharding import PartitionSpec as P

P_SIZE = 49
PV = 75
NPROBE = 16
LANES = 128
NORM_AT = PV
ALPHA_AT = PV + 3
FEATURES = 5
STRIDE = PV + FEATURES
TILES = (P_SIZE * STRIDE + 1 + 2 * NPROBE + LANES - 1) // LANES
PACKED = TILES * LANES
TAIL = PACKED - LANES
COUNT_AT = STRIDE
PROBE_AT = COUNT_AT + 1


def layout():
    rest, left = LANES - STRIDE, 2 * (LANES - STRIDE) - STRIDE
    pairs = TILES // 2
    places = [[(tile, 0, 0, STRIDE)] for tile in range(TILES)]
    places += [[(2 * k, STRIDE, 0, rest), (2 * k + 1, STRIDE, rest, STRIDE - rest)] for k in range(pairs)]
    each = STRIDE // left
    for j in range(P_SIZE - len(places)):
        places.append([(2 * (each * j + i) + 1, LANES - left, left * i, left) for i in range(each)])
    return places


OWNER_AT = STRIDE
ROWS = ((1792, 1), (2048, 1), (1024, None))
COLS = ((896, 2), (1024, None))
PREPARED = ((2048, None),)
FILL = 256
SCALE = 2.0 * math.log2(math.e) / (2.0 * PV)
NT = (((1,), (1,)), ((), ()))
NN = (((1,), (0,)), ((), ()))
VMEM = pl.BlockSpec(memory_space=pltpu.VMEM)
SMEM = pl.BlockSpec(memory_space=pltpu.SMEM)


def dot(a, b, dims=NN):
    return lax.dot_general(a, b, dims, preferred_element_type=jnp.float32)


def iota(shape, dim):
    return lax.broadcasted_iota(jnp.int32, shape, dim)


def parts(value):
    hi = value.astype(jnp.bfloat16).astype(jnp.float32)
    rest = value - hi
    mid = rest.astype(jnp.bfloat16).astype(jnp.float32)
    return hi, mid, (rest - mid).astype(jnp.bfloat16).astype(jnp.float32)


def pack_kernel(mine_ref, *refs):
    patches_ref, counts_ref, weights_ref, probes_ref, plan_ref, out_ref, met_ref = refs
    images, wide = patches_ref.shape
    cols, far = met_ref.shape
    plan = plan_ref[...]
    mine = mine_ref[0]
    partner = jnp.sum(jnp.where(iota(plan.shape, 1) == mine, plan, 0), axis=1, keepdims=True)
    line = iota((cols, far), 0)
    source = jnp.zeros((cols, far), jnp.int32)
    for meeting in range(plan.shape[0]):
        here = (line >= meeting * images) & (line < (meeting + 1) * images)
        apart = partner[meeting : meeting + 1, :] ^ mine
        slot = (apart & 1) * (far // images // 2) + (apart >> 1)
        source = jnp.where(here, slot * images + line - meeting * images, source)
    met_ref[...] = (iota((cols, far), 1) == source).astype(jnp.bfloat16)

    shape = (images, LANES)
    lane = iota(shape, 1)
    square = (images, images)
    along = jnp.broadcast_to(counts_ref[...].astype(jnp.float32), square)
    count = jnp.sum(jnp.where(iota(square, 0) == iota(square, 1), along, 0.0), axis=1, keepdims=True)
    weight = jnp.concatenate([weights_ref[...], jnp.zeros((1, LANES - P_SIZE), jnp.float32)], axis=1)
    alpha = weight * (lane.astype(jnp.float32) < count).astype(jnp.float32) / count
    patches = []
    for p in range(P_SIZE):
        values = patches_ref[:, p * PV : min(p * PV + LANES, wide)]
        if values.shape[1] < LANES:
            values = jnp.concatenate([values, jnp.zeros((images, LANES - values.shape[1]), jnp.bfloat16)], axis=1)
        patches.append(jnp.where(lane < PV, values, jnp.bfloat16(0)))
    stacked = jnp.concatenate(patches, axis=0).astype(jnp.float32)
    squares = stacked * stacked
    ones = jnp.ones((LANES, LANES), jnp.bfloat16)
    high = squares.astype(jnp.bfloat16)
    norm = dot(high, ones) + dot((squares - high.astype(jnp.float32)).astype(jnp.bfloat16), ones)
    norms = [part.astype(jnp.bfloat16) for part in parts(-0.5 * norm)]
    alphas = [part.astype(jnp.bfloat16) for part in parts(alpha)[:2]]
    tiles = [None] * (PACKED // LANES)

    def put(values, places):
        for tile, there, here, lanes in places:
            shift = (there - here) % LANES
            moved = pltpu.roll(values, shift, 1) if shift else values
            if lanes < LANES:
                moved = jnp.where((lane >= there) & (lane < there + lanes), moved, jnp.bfloat16(0))
            tiles[tile] = moved if tiles[tile] is None else tiles[tile] + moved

    places = layout()
    for p in range(P_SIZE):
        values = patches[p]
        for step, part in enumerate(norms):
            values = jnp.where(lane == NORM_AT + step, part[p * images : (p + 1) * images], values)
        for step, part in enumerate(alphas):
            values = jnp.where(lane == ALPHA_AT + step, pltpu.roll(part, (ALPHA_AT + step - p) % LANES, 1), values)
        put(values, places[p])
    probe_hi, probe_low, unused = parts(probes_ref[...])
    rest = jnp.concatenate(
        [count, probe_hi, probe_low, jnp.zeros((images, LANES - 1 - 2 * NPROBE), jnp.float32)], axis=1
    )
    put(rest.astype(jnp.bfloat16), [(TILES - 1, COUNT_AT, 0, LANES - STRIDE)])
    for tile, values in enumerate(tiles):
        out_ref[:, tile * LANES : (tile + 1) * LANES] = values


def pack(patches, counts, weights, probes, plan, mine):
    images = patches.shape[0]
    given = (patches, counts[None, :], weights[None, :], probes, plan)
    return pl.pallas_call(
        pack_kernel,
        out_shape=(
            jax.ShapeDtypeStruct((images, PACKED), jnp.bfloat16),
            jax.ShapeDtypeStruct((images * plan.shape[0], images * plan.shape[1]), jnp.bfloat16),
        ),
        in_specs=[SMEM] + [VMEM] * len(given),
        out_specs=(VMEM, VMEM),
        compiler_params=pltpu.CompilerParams(vmem_limit_bytes=8 * 2**20),
        name="pack",
    )(mine, *given)


def order(tail):
    number = tail.shape[0]
    count = tail[:, COUNT_AT : COUNT_AT + 1]
    key = count * number + (number - 1 - iota((number, 1), 0)).astype(jnp.float32)
    square = (number, number)
    key_here = jnp.broadcast_to(key, square)
    key_along = jnp.sum(jnp.where(iota(square, 0) == iota(square, 1), key_here, 0.0), axis=0, keepdims=True)
    rank = jnp.sum((key_here > key_along).astype(jnp.float32), axis=0, keepdims=True)
    chosen = (iota(square, 0).astype(jnp.float32) == rank).astype(jnp.bfloat16)
    patch = iota((number, LANES), 1).astype(jnp.float32)
    valid = jnp.sum((count > patch).astype(jnp.float32), axis=0, keepdims=True)
    before = (iota((LANES, LANES), 0) < iota((LANES, LANES), 1)).astype(jnp.bfloat16)
    first = dot(jnp.broadcast_to(valid, (8, LANES)).astype(jnp.bfloat16), before)
    return chosen, first.astype(jnp.int32)


def owners(chosen):
    number = chosen.shape[0]
    owner = jnp.sum(jnp.where(chosen > 0, iota((number, number), 1).astype(jnp.float32), 0.0), axis=1, keepdims=True)
    return jnp.where(iota((number, LANES), 1) == OWNER_AT, owner, 0.0)


def spread(sorted_ref, owner, first_ref, x_ref, options):
    number = sorted_ref.shape[0]
    lane = iota((number, LANES), 1)
    for p, places in enumerate(layout()):
        values = None
        for tile, there, here, lanes in places:
            moved = sorted_ref[:, tile * LANES : (tile + 1) * LANES]
            if there != here:
                moved = pltpu.roll(moved, (here - there) % LANES, 1)
            values = moved if values is None else jnp.where(lane < here, values, moved)
        values = jnp.where(lane < STRIDE, values.astype(jnp.float32), owner)
        x_ref[pl.ds(first_ref[0, p], number), :] = values
    total = first_ref[0, P_SIZE]
    counts = choose(total, options)
    end = sum(count * size for count, (size, unused) in zip(counts, options))

    def clear(step, unused):
        x_ref[pl.ds(total + step * FILL, FILL), :] = jnp.zeros((FILL, LANES), jnp.float32)
        return unused

    lax.fori_loop(0, (end - total + FILL - 1) // FILL, clear, 0)
    return total, counts


def choose(total, options):
    counts, left = [], 1
    for size, most in options:
        need = (total + size - 1) // size
        fits = left if most is None else jnp.where(need <= most, left, 0)
        counts.append(fits * need)
        left = left - fits
    return counts


def cover(counts, options, step, carry):
    for count, (size, unused) in zip(counts, options):
        carry = lax.fori_loop(0, count, lambda k, c, size=size: step(pl.multiple_of(k * size, LANES), size, c), carry)
    return carry


def rank_rows_kernel(*refs):
    chosen_ref, first_ref = refs[-2:]
    tail = jnp.concatenate([part[:, TAIL : TAIL + LANES] for part in refs[:-2]], axis=0)
    chosen_ref[...], first_ref[...] = order(tail.astype(jnp.float32))


def rank_cols_kernel(met_ref, *refs):
    chosen_ref, first_ref, which_ref, tail_ref = refs[-4:]
    met = met_ref[...]
    tail = dot(met, jnp.concatenate([part[:, TAIL : TAIL + LANES] for part in refs[:-4]], axis=0))
    tail_ref[...] = tail.astype(jnp.bfloat16)
    chosen_ref[...], first_ref[...] = order(tail)
    which_ref[...] = dot(chosen_ref[...], met).astype(jnp.bfloat16)


def rank(kernel, given, number, more, flops):
    shapes = (
        jax.ShapeDtypeStruct((number, number), jnp.bfloat16),
        jax.ShapeDtypeStruct((8, LANES), jnp.int32),
    ) + tuple(jax.ShapeDtypeStruct(shape, jnp.bfloat16) for shape in more)
    return pl.pallas_call(
        kernel,
        out_shape=shapes,
        in_specs=[VMEM] * len(given),
        out_specs=(VMEM,) * len(shapes),
        compiler_params=pltpu.CompilerParams(vmem_limit_bytes=8 * 2**20),
        cost_estimate=pl.CostEstimate(flops=flops, bytes_accessed=10**6, transcendentals=0),
        name="rank",
    )(*given)


def energies(counted, *refs):
    near_number, far_number = counted
    row_given, col_given, row_order, col_order, col_which, tail_ref = refs[:6]
    near_parts = refs[6 : 6 + near_number]
    far_parts = refs[6 + near_number : 6 + near_number + far_number]
    (out_ref, row_sorted, col_sorted, row_x, col_f, col_x, col_u, product, row_first, col_first, sem) = refs[
        6 + near_number + far_number :
    ]
    cols = col_order.shape[0]
    copies = [pltpu.make_async_copy(s, t, sem.at[k]) for k, (s, t) in enumerate(((col_given, col_first), (row_given, row_first)))]
    for copy in copies:
        copy.start()
    product[...] = jnp.zeros_like(product)
    col_sorted[...] = dot(col_which[...], jnp.concatenate([part[...] for part in far_parts], axis=0)).astype(jnp.bfloat16)
    row_sorted[...] = dot(row_order[...], jnp.concatenate([part[...] for part in near_parts], axis=0)).astype(jnp.bfloat16)
    both = (2 * NPROBE, LANES)
    pick_probe = (iota(both, 1) == iota(both, 0) + PROBE_AT).astype(jnp.bfloat16)
    probes = dot(pick_probe, tail_ref[...], NT).astype(jnp.bfloat16)
    col_owner, row_owner = owners(col_order[...]), owners(row_order[...])
    copies[0].wait()
    col_total, col_counts = spread(col_sorted, col_owner, col_first, col_f, COLS)
    copies[1].wait()
    row_total, row_counts = spread(row_sorted, row_owner, row_first, row_x, ROWS)

    line, lane = iota((NPROBE, LANES), 0), iota((NPROBE, LANES), 1)
    pick = (
        ((line == 0) & (lane >= NORM_AT) & (lane < ALPHA_AT))
        | ((line == 1) & (lane >= ALPHA_AT) & (lane < STRIDE))
        | ((line == 2) & (lane == OWNER_AT))
    ).astype(jnp.bfloat16)
    def owned(picked, number, size):
        return (iota((number, size), 0).astype(jnp.float32) == picked[2:3]).astype(jnp.bfloat16)

    def prepare(start, size, unused):
        here = pl.ds(start, size)
        x_cols = col_f[here, :].astype(jnp.bfloat16)
        col_x[here, :] = x_cols
        picked = dot(pick, x_cols, NT)
        mine = dot(probes, owned(picked, cols, size))
        col_u[:, here] = (picked[1:2] * (mine[:NPROBE] + mine[NPROBE:])).astype(jnp.bfloat16)
        return unused

    cover(choose(col_total, PREPARED), PREPARED, prepare, 0)

    def one_row(start, size, unused):
        x_rows = row_x[pl.ds(start, size), :].astype(jnp.bfloat16)
        picked = dot(pick, x_rows, NT)
        row_lane = iota((size, LANES), 1)
        x_rows = jnp.where(
            row_lane < NORM_AT, x_rows, jnp.where(row_lane < ALPHA_AT, jnp.bfloat16(1), jnp.bfloat16(0))
        )

        def one_col(start, size, total):
            here = pl.ds(start, size)
            inner = dot(col_x[here, :], x_rows, NT)
            energy = jnp.exp2((inner + picked[0:1]) * SCALE).astype(jnp.bfloat16)
            return total + dot(col_u[:, here], energy)

        total = cover(col_counts, COLS, one_col, jnp.zeros((NPROBE, size), jnp.float32))
        weighted = jnp.concatenate(parts(total * picked[1:2]), axis=0).astype(jnp.bfloat16)
        sums = dot(weighted, owned(picked, product.shape[1], size), NT)
        product[...] += sums[0:NPROBE] + sums[NPROBE : 2 * NPROBE] + sums[2 * NPROBE :]
        return unused

    cover(row_counts, ROWS, one_row, 0)
    out_ref[...] = product[...].T


def local_terms(rows_rank, cols_rank, near, far):
    row_order, row_first = rows_rank
    col_order, col_first, col_which, col_tail = cols_rank
    rows, cols = row_order.shape[0], col_order.shape[0]
    row_room = rows * P_SIZE + ROWS[1][0] + FILL
    col_room = (cols * P_SIZE // PREPARED[0][0] + 1) * PREPARED[0][0] + FILL
    return pl.pallas_call(
        functools.partial(energies, (len(near), len(far))),
        out_shape=jax.ShapeDtypeStruct((rows, NPROBE), jnp.float32),
        in_specs=[VMEM] * (6 + len(near) + len(far)),
        out_specs=VMEM,
        scratch_shapes=[
            pltpu.VMEM((rows, PACKED), jnp.bfloat16),
            pltpu.VMEM((cols, PACKED), jnp.bfloat16),
            pltpu.VMEM((row_room, LANES), jnp.float32),
            pltpu.VMEM((col_room, LANES), jnp.float32),
            pltpu.VMEM((col_room, LANES), jnp.bfloat16),
            pltpu.VMEM((NPROBE, col_room), jnp.bfloat16),
            pltpu.VMEM((NPROBE, rows), jnp.float32),
            pltpu.SMEM((8, LANES), jnp.int32),
            pltpu.SMEM((8, LANES), jnp.int32),
            pltpu.SemaphoreType.DMA((2,)),
        ],
        compiler_params=pltpu.CompilerParams(vmem_limit_bytes=40 * 2**20),
        name="energies",
    )(row_first, col_first, row_order, col_order, col_which, col_tail, *near, *far)


def shards(patches, counts, weights, probes, plan):
    images = patches.shape[0]
    mine = lax.axis_index("group").reshape(1)
    packed, met = pack(patches, counts, weights, probes, plan, mine)
    groups, subs = lax.axis_size("group"), lax.axis_size("narrow")

    def swap(array, apart):
        return lax.ppermute(array, "group", [(i, i ^ apart) for i in range(groups)])

    def across(array, apart):
        return lax.ppermute(array, "narrow", [(i, i ^ apart) for i in range(subs)])

    even = [packed] + [swap(packed, apart) for apart in range(groups - 2, 0, -2)][::-1]
    far = even + [swap(array, 1) for array in even]
    near = [packed]
    for apart in range(1, subs):
        low = apart & -apart
        near.append(across(near[apart - low], low))
    rows_rank = rank(rank_rows_kernel, near, subs * images, (), 20 * 10**9)
    cols = met.shape[0]
    cols_rank = rank(rank_cols_kernel, [met, *far], cols, (met.shape, (cols, LANES)), 2 * 10**9)
    terms = local_terms(rows_rank, cols_rank, near, far)
    total = terms[:images]
    for apart in (subs - 1, *range(1, subs - 1)):
        total = total + across(terms[apart * images : (apart + 1) * images], apart)
    return total


def solution(mesh):
    return jax.shard_map(
        shards,
        mesh=mesh,
        in_specs=(
            P(("group", "narrow"), None),
            P(("group", "narrow")),
            P(),
            P(("group", "narrow"), None),
            P(),
        ),
        out_specs=P(("group", "narrow"), None),
        check_vma=False,
    )
```
